512 devices in a mesh: rep: 32 (over z_lo, y), fsdp: 16 (over z_hi, x, core).
Axes of the slice: x: 4, y: 8, z: 8 (z_hi: 2, z_lo: 4; z = z_hi * 4 + z_lo), core: 2. Of those that a mesh axis runs over, the one named last changes fastest.
Arguments:
- inputs: bfloat16 [32, 2048, 4096], P('rep', 'fsdp'), may hold values from -6 to 6
- key_grads: bfloat16 [32, 2048, 512], P('rep', 'fsdp'), may hold values from -0.3125 to 0.3125
- weights: float32 [32, 4096, 512], P('rep', 'fsdp'), may hold values from -0.09375 to 0.09375
- first_moment: bfloat16 [32, 4096, 512], P('rep', 'fsdp'), may hold values from -1.25 to 1.25
- second_moment: bfloat16 [32, 4096, 512], P('rep', 'fsdp'), may hold values from 0.099609375 to 1
- drift: float32 [32, 4096, 512], P('rep', 'fsdp'), may hold values from -0.125 to 0.125
- momentum: float32 [4096, 512], P(('fsdp', 'rep')), may hold values from -0.0625 to 0.0625
- global_weights: float32 [4096, 512], P(('fsdp', 'rep')), may hold values from -0.09375 to 0.09375
Outputs:
- keys: bfloat16 [32, 2048, 512], P('rep', 'fsdp')
- input_grads: bfloat16 [32, 2048, 4096], P('rep', 'fsdp')
- merged_weights: float32 [32, 4096, 512], P('rep', 'fsdp')
- new_first_moment: bfloat16 [32, 4096, 512], P('rep', 'fsdp')
- new_second_moment: bfloat16 [32, 4096, 512], P('rep', 'fsdp')
- new_momentum: float32 [4096, 512], P(('fsdp', 'rep'))
- new_global: float32 [4096, 512], P(('fsdp', 'rep'))
The draws below stay inside these ranges and needn't reach their ends.
All inputs are finite; a program needn't handle non-finite values.
Results may differ from the reference program's by a relative error of at most 0.02.
Values may be sent and summed in bfloat16 or wider, within the bound.
A program may use at most 64 MiB of HBM per device.

```python
import math
import jax
import jax.numpy as jnp
from jax import lax

D_WIN = 4096
HEAD = 128
SEQ = 1024
TOK_DEV = 128
KV_COLS = 512
TOK_REP = 2048
N_REP = 32
N_FSDP = 16


def spiked(drawn, key, source, target, blocks, factor):
    owner, partner = [(jnp.arange(drawn.shape[axis_at]) // (drawn.shape[axis_at] // blocks)).reshape([-1 if axis == axis_at else 1 for axis in range(drawn.ndim)]) for axis_at in (source, target)]
    chosen = jax.random.permutation(key, blocks)[partner]
    strong = (owner == chosen) | (owner == (partner + blocks // 2) % blocks)
    return jnp.where(strong, factor * drawn, drawn)


def block_scale(own_key, dims, pieces, least, largest):
    loudness, own = 1.0, jax.random.fold_in(own_key, 6)
    for axis_at, shards_of in pieces:
        draws = jnp.exp(jax.random.uniform(jax.random.fold_in(own, axis_at), (shards_of,), jnp.float32, least / len(pieces), largest / len(pieces)))
        loudness = loudness * jnp.repeat(draws, dims[axis_at] // shards_of).reshape([-1 if axis == axis_at else 1 for axis in range(len(dims))])
    return loudness


def normal_values(own_key, dims, scale, reach, pieces=(), kind=jnp.bfloat16):
    values = jax.random.normal(own_key, dims, jnp.float32) * scale
    if len(pieces) > 0:
        values = block_scale(own_key, dims, pieces, -0.22, 0.18) * values
    return jnp.clip(values, min=-reach, max=reach).astype(kind)


def noise_with(own_key, dims, width, limit, cuts, heavy, kind=jnp.bfloat16):
    values = width * jax.random.normal(own_key, dims, jnp.float32)
    if cuts:
        values = values * block_scale(own_key, dims, cuts, -0.22, 0.18)
    return jnp.clip(spiked(values, jax.random.fold_in(own_key, 3), *heavy), -limit, limit).astype(kind)


def setup_inputs(seed: int = 0) -> dict:
    splits = jax.random.split(jax.random.key(seed), 9)
    return {
        "inputs": normal_values(splits[0], (N_REP, TOK_REP, D_WIN), 1.0, 6.0, ((0, 32), (1, 16))),
        "key_grads": normal_values(splits[1], (N_REP, TOK_REP, KV_COLS), 0.05, 0.3125, ((0, 32), (1, 16))),
        "weights": normal_values(splits[2], (N_REP, D_WIN, KV_COLS), D_WIN ** -0.5, 0.09375, ((0, 32), (1, 16)), jnp.float32),
        "first_moment": normal_values(splits[3], (N_REP, D_WIN, KV_COLS), 0.2, 1.25, ((0, 32), (1, 16))),
        "second_moment": jnp.clip(jnp.exp(math.log(1.0) - 2.306499 * jax.random.uniform(splits[4], (N_REP, D_WIN, KV_COLS), jnp.float32) ** block_scale(splits[4], (N_REP, D_WIN, KV_COLS), ((0, 32), (1, 16)), -0.2, 0.2)), 0.099609375, 1.0).astype(jnp.bfloat16),
        "drift": noise_with(splits[5], (N_REP, D_WIN, KV_COLS), 0.01, 0.125, ((0, 32), (1, 16)), (0, 1, 32, 2.75), jnp.float32),
        "momentum": normal_values(splits[6], (D_WIN, KV_COLS), 0.01, 0.0625, ((0, 512),), jnp.float32),
        "global_weights": normal_values(splits[7], (D_WIN, KV_COLS), D_WIN ** -0.5, 0.09375, ((0, 512),), jnp.float32),
    }


learning_rate = 0.002
beta_one = 0.9
beta_two = 0.95
adam_epsilon = 1e-08
weight_decay = 0.1
outer_rate = 0.7
outer_beta = 0.9
mixing = 0.5
rope_base = 500000.0

def rope_tables(positions):
    half_size = HEAD // 2
    exponents = jnp.arange(half_size, dtype=jnp.float32) * (2.0 / HEAD)
    inverse_freq = jnp.power(jnp.float32(rope_base), -exponents)
    angles = positions[:, None] * inverse_freq[None, :]
    return (jnp.cos(angles)[:, None, :], jnp.sin(angles)[:, None, :])

def rotate(values, cosine, sines, sign):
    shape = values.shape
    heads = values.reshape(shape[0], shape[1] // HEAD, HEAD)
    half_size = HEAD // 2
    first = heads[..., :half_size]
    second = heads[..., half_size:]
    out_first = first * cosine - sign * second * sines
    out_second = second * cosine + sign * first * sines
    return jnp.concatenate([out_first, out_second], axis=-1).reshape(shape)

def reference(inputs, key_grads, weights, first_moment, second_moment, drift, momentum, global_weights):
    mean_drift = lax.optimization_barrier(jnp.sum(drift, axis=0)) / N_REP
    new_momentum = outer_beta * momentum + mean_drift
    new_global = global_weights - outer_rate * (mean_drift + outer_beta * new_momentum)
    positions = (jnp.arange(TOK_REP) % SEQ).astype(jnp.float32)
    cosine, sines = rope_tables(positions)

    def partial_term(pair):
        return jnp.dot(pair[0].T, pair[1], preferred_element_type=jnp.float32).astype(jnp.bfloat16)

    def one_replica(items):
        tokens, grads, master, first, second = items
        low = master.astype(jnp.bfloat16)
        projected = jnp.dot(tokens, low, preferred_element_type=jnp.float32)
        rotated = rotate(projected, cosine, sines, 1.0).astype(jnp.bfloat16)
        unrotated = rotate(grads.astype(jnp.float32), cosine, sines, -1.0).astype(jnp.bfloat16)
        backward = jnp.dot(unrotated, low.T, preferred_element_type=jnp.float32).astype(jnp.bfloat16)
        token_parts = tokens.reshape(N_FSDP, TOK_DEV, D_WIN)
        grad_parts = unrotated.reshape(N_FSDP, TOK_DEV, KV_COLS)
        partials = lax.map(partial_term, (token_parts, grad_parts))
        gradient = lax.optimization_barrier(jnp.sum(partials.astype(jnp.float32), axis=0))
        moment_one = beta_one * first.astype(jnp.float32) + (1.0 - beta_one) * gradient
        moment_two = beta_two * second.astype(jnp.float32) + (1.0 - beta_two) * gradient * gradient
        stepped = master - learning_rate * (moment_one / (jnp.sqrt(moment_two) + adam_epsilon) + weight_decay * master)
        merged = mixing * stepped + (1.0 - mixing) * new_global
        return (rotated, backward, merged, moment_one.astype(jnp.bfloat16), moment_two.astype(jnp.bfloat16))
    keys, input_grads, merged_weights, first_out, second_out = lax.map(one_replica, (inputs, key_grads, weights, first_moment, second_moment))
    return (keys, input_grads, merged_weights, first_out, second_out, new_momentum, new_global)
```

```python
import functools

import jax
import jax.numpy as jnp
import numpy as np
from jax import lax
from jax.experimental import pallas as pl
from jax.experimental.pallas import tpu as pltpu
from jax.sharding import PartitionSpec as P

HEAD = 128
SEQ = 1024
TOK = 128
ROWS = 256
COLS = 512
WIN = 4096
N_REP = 32
N_X = 4
N_Y = 8
N_ZL = 4

learning_rate = 0.002
beta_one = 0.9
beta_two = 0.95
adam_epsilon = 1e-08
weight_decay = 0.1
outer_rate = 0.7
outer_beta = 0.9
mixing = 0.5
rope_base = 500000.0

F32 = jnp.float32
BF16 = jnp.bfloat16
MESH = pl.DeviceIdType.MESH


def rotary_tables():
    half = HEAD // 2
    freq = rope_base ** (-np.arange(half, dtype=np.float64) * (2.0 / HEAD))
    angles = np.arange(SEQ, dtype=np.float64)[:, None] * freq[None, :]
    cosine, sines = np.cos(angles), np.sin(angles)
    first = np.concatenate([cosine, cosine], axis=1)
    second = np.concatenate([-sines, sines], axis=1)
    both = np.stack([first, second]).astype(np.float32)
    return both.reshape(2, SEQ // TOK, TOK, HEAD).transpose(1, 0, 2, 3).copy()


def rotated_heads(values, tables, sign):
    cosine = tables[0]
    sines = sign * tables[1]
    heads = []
    for head in range(COLS // HEAD):
        part = values[:, head * HEAD : (head + 1) * HEAD]
        heads.append(part * cosine + pltpu.roll(part, HEAD // 2, 1) * sines)
    return jnp.concatenate(heads, axis=1)


REMOTE = (
    ("u", 3), ("ap", 3), ("ao", 3), ("igo", 3), ("igp", 3), ("pk", 3),
    ("wsib", 1), ("wz", 1), ("wfwd", 1), ("gpsib", 1), ("gosib", 1), ("gz", 1),
    ("dy", 7), ("dz", 3), ("az", 3), ("ay", 7),
)
LOCAL = (
    "kg", "tab", "w", "m1", "m2", "mo", "gl", "ap", "ao", "dr",
    "igo", "igp", "mg", "m1o", "m2o", "nm", "ng", "keys",
)
FIRST = {}
N_REMOTE = 0
for _name, _count in REMOTE:
    FIRST[_name] = N_REMOTE
    N_REMOTE += _count


def kernel(
    inp, kg, wt, m1, m2, dr, mo, gl, tab,
    keys_out, ig_out, mg_out, m1_out, m2_out, nm_out, ng_out,
    kg_v, tab_v, w_v, m1_v, m2_v, mo_v, gl_v,
    u_all, ap, ao, w_o, w_p, ig_o, ig_p, pk_send, pk_recv, pk_own,
    gp, go, gp_send, gp_recv, go_send, go_recv, gz_send, gz_recv,
    dr_all, ds, dz, ga, gg, nm_v, mg_v, m1o_v, m2o_v, keys_v,
    send_sem, recv_sem, local_sem,
):
    rep = lax.axis_index("rep")
    fsdp = lax.axis_index("fsdp")
    zl, y = rep // N_Y, rep % N_Y
    zh, x, core = fsdp // 8, (fsdp // 2) % N_X, fsdp % 2

    def at_x(step):
        return (rep, zh * 8 + ((x + step) % N_X) * 2 + core)

    def at_y(step):
        return (zl * N_Y + (y + step) % N_Y, fsdp)

    def at_zl(step):
        return (((zl + step) % N_ZL) * N_Y + y, fsdp)

    sibling = (rep, zh * 8 + x * 2 + (1 - core))
    partner = (rep, (1 - zh) * 8 + x * 2 + core)

    def remote(name, index, src, dst, device):
        at = FIRST[name] + index
        return pltpu.make_async_remote_copy(
            src_ref=src, dst_ref=dst, send_sem=send_sem.at[at], recv_sem=recv_sem.at[at],
            device_id=device, device_id_type=MESH,
        )

    def local(name, src, dst):
        return pltpu.make_async_copy(src, dst, local_sem.at[LOCAL.index(name)])

    barrier = pltpu.get_barrier_semaphore()
    peers = [sibling, partner] + [at_x(d) for d in (1, 2, 3)]
    peers += [at_y(e) for e in range(1, N_Y)] + [at_zl(f) for f in range(1, N_ZL)]
    for device in peers:
        pl.semaphore_signal(barrier, inc=1, device_id=device, device_id_type=MESH)

    own_rows = pl.ds(core * ROWS, ROWS)
    sib_rows = pl.ds((1 - core) * ROWS, ROWS)

    def columns(half, chip):
        return pl.ds(pl.multiple_of(half * (WIN // 2) + chip * COLS, COLS), COLS)

    def slot(d):
        return pl.ds(d * TOK, TOK)

    loads = {
        "kg": local("kg", kg.at[0], kg_v),
        "tab": local("tab", tab.at[fsdp % 8], tab_v),
        "w": local("w", wt.at[0], w_v),
        "ap": local("ap", inp.at[0, :, columns(1 - zh, x)], ap.at[slot(0)]),
        "ao": local("ao", inp.at[0, :, columns(zh, x)], ao.at[slot(0)]),
        "dr": local("dr", dr.at[:, y], dr_all.at[0]),
        "m1": local("m1", m1.at[0], m1_v),
        "m2": local("m2", m2.at[0], m2_v),
        "mo": local("mo", mo, mo_v),
        "gl": local("gl", gl, gl_v),
    }
    for copy in loads.values():
        copy.start()

    loads["kg"].wait()
    loads["tab"].wait()
    tables = (tab_v[0], tab_v[1])
    u_all[slot(0), :] = rotated_heads(kg_v[...].astype(F32), tables, -1.0).astype(BF16)
    loads["w"].wait()
    w_o[own_rows, :] = w_v[...].astype(BF16)

    pl.semaphore_wait(barrier, len(peers))

    wz = remote("wz", 0, w_o.at[own_rows], w_p.at[own_rows], partner)
    wsib = remote("wsib", 0, w_o.at[own_rows], w_o.at[own_rows], sibling)
    wz.start()
    wsib.start()
    xs = (1, 3, 2)
    u_copy = {d: remote("u", d - 1, u_all.at[slot(0)], u_all.at[slot(d)], at_x(d)) for d in xs}
    ap_copy = {
        d: remote("ap", d - 1, inp.at[0, :, columns(1 - zh, (x + d) % N_X)], ap.at[slot(d)], at_x(d))
        for d in xs
    }
    ao_copy = {
        d: remote("ao", d - 1, inp.at[0, :, columns(zh, (x + d) % N_X)], ao.at[slot(d)], at_x(d))
        for d in xs
    }
    dy_copy = {
        e: remote("dy", e - 1, dr.at[:, (y + e) % N_Y], dr_all.at[e], at_y(e))
        for e in range(1, N_Y)
    }
    for copies in (u_copy, ap_copy, dy_copy, ao_copy):
        for copy in copies.values():
            copy.start()

    wsib.wait_recv()
    for copy in u_copy.values():
        copy.wait_recv()
    ig_o[...] = lax.dot_general(
        u_all[...], w_o[...], (((1,), (1,)), ((), ())), preferred_element_type=F32
    ).astype(BF16)
    igo_copy = {
        d: remote("igo", d - 1, ig_o.at[slot(d)], ig_out.at[0, :, columns(zh, x)], at_x(4 - d))
        for d in xs
    }
    for copy in igo_copy.values():
        copy.start()
    outs = [local("igo", ig_o.at[slot(0)], ig_out.at[0, :, columns(zh, x)])]
    outs[0].start()

    loads["dr"].wait()
    for copy in dy_copy.values():
        copy.wait_recv()
    total = dr_all[0]
    for e in range(1, N_Y):
        total = total + dr_all[e]
    ds[...] = total
    dz_copy = {
        f: remote("dz", f - 1, ds.at[(zl + f) % N_ZL], dz.at[f - 1], at_zl(f))
        for f in range(1, N_ZL)
    }
    for copy in dz_copy.values():
        copy.start()

    loads["ap"].wait()
    for copy in ap_copy.values():
        copy.wait_recv()
    gp[...] = lax.dot_general(
        ap[...], u_all[...], (((0,), (0,)), ((), ())), preferred_element_type=F32
    )
    gp_send[...] = gp[sib_rows, :].astype(BF16)
    gpsib = remote("gpsib", 0, gp_send, gp_recv, sibling)
    gpsib.start()

    wz.wait_recv()
    wfwd = remote("wfwd", 0, w_p.at[own_rows], w_p.at[own_rows], sibling)
    wfwd.start()

    gpsib.wait_recv()
    gz_send[...] = (gp[own_rows, :] + gp_recv[...].astype(F32)).astype(BF16)
    gz = remote("gz", 0, gz_send, gz_recv, partner)
    gz.start()

    wfwd.wait_recv()
    ig_p[...] = lax.dot_general(
        u_all[...], w_p[...], (((1,), (1,)), ((), ())), preferred_element_type=F32
    ).astype(BF16)
    igp_copy = {
        d: remote("igp", d - 1, ig_p.at[slot(d)], ig_out.at[0, :, columns(1 - zh, x)], at_x(4 - d))
        for d in xs
    }
    for copy in igp_copy.values():
        copy.start()
    outs.append(local("igp", ig_p.at[slot(0)], ig_out.at[0, :, columns(1 - zh, x)]))
    outs[-1].start()

    loads["mo"].wait()
    loads["gl"].wait()
    for copy in dz_copy.values():
        copy.wait_recv()
    mean_drift = (ds[zl] + dz[0] + dz[1] + dz[2]) / N_REP
    moment = outer_beta * mo_v[...] + mean_drift
    nm_v[...] = moment
    ga[zl] = gl_v[...] - outer_rate * (mean_drift + outer_beta * moment)
    az_copy = {
        f: remote("az", f - 1, ga.at[zl], ga.at[zl], at_zl(f)) for f in range(1, N_ZL)
    }
    for copy in az_copy.values():
        copy.start()
    outs.append(local("nm", nm_v, nm_out))
    outs[-1].start()
    outs.append(local("ng", ga.at[zl], ng_out))
    outs[-1].start()

    loads["ao"].wait()
    for copy in ao_copy.values():
        copy.wait_recv()
    for d in (1, 3, 2, 0):
        part = jnp.dot(ao[slot(d), :], w_o[...], preferred_element_type=F32)
        part += jnp.dot(ap[slot(d), :], w_p[...], preferred_element_type=F32)
        if d == 0:
            pk_own[...] = part
        else:
            pk_send[d - 1] = part.astype(BF16)
    pk_copy = {
        d: remote("pk", d - 1, pk_send.at[d - 1], pk_recv.at[d - 1], at_x(4 - d)) for d in xs
    }
    for copy in pk_copy.values():
        copy.start()

    for copy in az_copy.values():
        copy.wait_recv()
    ay_copy = {
        e: remote("ay", e - 1, ga, gg.at[:, y], at_y(e)) for e in range(1, N_Y)
    }
    for copy in ay_copy.values():
        copy.start()
    gg[:, y] = ga[...]

    go[...] = lax.dot_general(
        ao[...], u_all[...], (((0,), (0,)), ((), ())), preferred_element_type=F32
    )
    go_send[...] = go[sib_rows, :].astype(BF16)
    gosib = remote("gosib", 0, go_send, go_recv, sibling)
    gosib.start()

    loads["m1"].wait()
    loads["m2"].wait()
    gosib.wait_recv()
    for copy in ay_copy.values():
        copy.wait_recv()
    gz.wait_recv()

    own = core * ROWS
    for zone in range(N_ZL):
        rows = pl.ds(zone * 64, 64)
        gradient = (
            go[pl.ds(own + zone * 64, 64), :]
            + go_recv[rows, :].astype(F32)
            + gz_recv[rows, :].astype(F32)
        )
        master = w_v[rows, :]
        moment_one = beta_one * m1_v[rows, :].astype(F32) + (1.0 - beta_one) * gradient
        moment_two = (
            beta_two * m2_v[rows, :].astype(F32) + (1.0 - beta_two) * gradient * gradient
        )
        stepped = master - learning_rate * (
            moment_one / (jnp.sqrt(moment_two) + adam_epsilon) + weight_decay * master
        )
        mg_v[rows, :] = mixing * stepped + (1.0 - mixing) * gg[zone].reshape(64, COLS)
        m1o_v[rows, :] = moment_one.astype(BF16)
        m2o_v[rows, :] = moment_two.astype(BF16)
    for name, src, dst in (("mg", mg_v, mg_out), ("m1o", m1o_v, m1_out), ("m2o", m2o_v, m2_out)):
        outs.append(local(name, src, dst.at[0]))
        outs[-1].start()

    for copy in pk_copy.values():
        copy.wait_recv()
    projected = pk_own[...]
    for d in range(3):
        projected = projected + pk_recv[d].astype(F32)
    keys_v[...] = rotated_heads(projected, tables, 1.0).astype(BF16)
    outs.append(local("keys", keys_v, keys_out.at[0]))
    outs[-1].start()

    for copies in (igo_copy, igp_copy):
        for copy in copies.values():
            copy.wait_recv()
    for copies in (u_copy, ap_copy, ao_copy, dy_copy, igo_copy, igp_copy, dz_copy, az_copy, ay_copy, pk_copy):
        for copy in copies.values():
            copy.wait_send()
    for copy in (wz, wsib, wfwd, gpsib, gosib, gz):
        copy.wait_send()
    for copy in outs:
        copy.wait()


def body(inputs, key_grads, weights, first_moment, second_moment, drift, momentum, global_weights):
    shape = jax.ShapeDtypeStruct
    vmem = pltpu.VMEM
    big = (4 * TOK, COLS)
    piece = (N_ZL, 8, COLS)
    scratch = [
        vmem((TOK, COLS), BF16), vmem((2, TOK, HEAD), F32), vmem((ROWS, COLS), F32),
        vmem((ROWS, COLS), BF16), vmem((ROWS, COLS), BF16), vmem((8, COLS), F32), vmem((8, COLS), F32),
        vmem(big, BF16), vmem(big, BF16), vmem(big, BF16), vmem(big, BF16), vmem(big, BF16),
        vmem(big, BF16), vmem(big, BF16),
        vmem((3, TOK, COLS), BF16), vmem((3, TOK, COLS), BF16), vmem((TOK, COLS), F32),
        vmem(big, F32), vmem(big, F32),
        vmem((ROWS, COLS), BF16), vmem((ROWS, COLS), BF16), vmem((ROWS, COLS), BF16),
        vmem((ROWS, COLS), BF16), vmem((ROWS, COLS), BF16), vmem((ROWS, COLS), BF16),
        vmem((N_Y,) + piece, F32), vmem(piece, F32), vmem((3, 8, COLS), F32), vmem(piece, F32),
        vmem((N_ZL, N_Y, 8, COLS), F32), vmem((8, COLS), F32), vmem((ROWS, COLS), F32),
        vmem((ROWS, COLS), BF16), vmem((ROWS, COLS), BF16), vmem((TOK, COLS), BF16),
        pltpu.SemaphoreType.DMA((N_REMOTE,)), pltpu.SemaphoreType.DMA((N_REMOTE,)),
        pltpu.SemaphoreType.DMA((len(LOCAL),)),
    ]
    outs = (
        shape((1, TOK, COLS), BF16), shape((1, TOK, WIN), BF16), shape((1, ROWS, COLS), F32),
        shape((1, ROWS, COLS), BF16), shape((1, ROWS, COLS), BF16),
        shape((8, COLS), F32), shape((8, COLS), F32),
    )
    anywhere = pl.BlockSpec(memory_space=pl.ANY)
    return pl.pallas_call(
        kernel,
        out_shape=outs,
        in_specs=[anywhere] * 9,
        out_specs=[anywhere] * 7,
        scratch_shapes=scratch,
        compiler_params=pltpu.CompilerParams(
            collective_id=0, has_side_effects=True, vmem_limit_bytes=56 * 2**20
        ),
    )(
        inputs, key_grads, weights, first_moment, second_moment,
        drift.reshape(N_ZL, N_Y, 8, COLS), momentum, global_weights, jnp.asarray(rotary_tables()),
    )


def solution(mesh):
    split = P("rep", "fsdp", None)
    rows = P(("fsdp", "rep"), None)
    return jax.shard_map(
        body,
        mesh=mesh,
        in_specs=(split,) * 6 + (rows,) * 2,
        out_specs=(split,) * 5 + (rows,) * 2,
        check_vma=False,
    )
```

```python
import functools

import jax
import jax.numpy as jnp
import numpy as np
from jax import lax
from jax.experimental import pallas as pl
from jax.experimental.pallas import tpu as pltpu
from jax.sharding import PartitionSpec as P

HEAD = 128
SEQ = 1024
TOK = 128
ROWS = 256
COLS = 512
WIN = 4096
N_REP = 32
N_X = 4
N_Y = 8
N_ZL = 4

learning_rate = 0.002
beta_one = 0.9
beta_two = 0.95
adam_epsilon = 1e-08
weight_decay = 0.1
outer_rate = 0.7
outer_beta = 0.9
mixing = 0.5
rope_base = 500000.0

F32 = jnp.float32
BF16 = jnp.bfloat16
MESH = pl.DeviceIdType.MESH


def rotary_tables():
    half = HEAD // 2
    freq = rope_base ** (-np.arange(half, dtype=np.float64) * (2.0 / HEAD))
    angles = np.arange(SEQ, dtype=np.float64)[:, None] * freq[None, :]
    cosine, sines = np.cos(angles), np.sin(angles)
    first = np.concatenate([cosine, cosine], axis=1)
    second = np.concatenate([-sines, sines], axis=1)
    both = np.stack([first, second]).astype(np.float32)
    return both.reshape(2, SEQ // TOK, TOK, HEAD).transpose(1, 0, 2, 3).copy()


def rotated_heads(values, tables, sign):
    cosine = tables[0]
    sines = sign * tables[1]
    heads = []
    for head in range(COLS // HEAD):
        part = values[:, head * HEAD : (head + 1) * HEAD]
        heads.append(part * cosine + pltpu.roll(part, HEAD // 2, 1) * sines)
    return jnp.concatenate(heads, axis=1)


REMOTE = (
    ("u", N_X), ("ap", N_X), ("ao", N_X), ("igo", N_X), ("igp", N_X), ("pk", N_X),
    ("wsib", 1), ("wz", 1), ("wfwd", 1), ("gpsib", 1), ("gosib", 1), ("gz", 1),
    ("dy", 7), ("dz", 3), ("base", 3), ("ay", 7),
)
LOCAL = (
    "kg", "tab", "w", "m1", "m2", "mo", "gl", "ap", "ao", "dr",
    "igo", "igp", "mg", "m1o", "m2o", "nm", "ng", "keys",
)
FIRST = {}
N_REMOTE = 0
for _name, _count in REMOTE:
    FIRST[_name] = N_REMOTE
    N_REMOTE += _count
MET_SIB, MET_Z, MET_Y, MET_ZL = N_X, N_X + 1, N_X + 2, N_X + 3


def kernel(
    inp, kg, wt, m1, m2, dr, mo, gl, tab,
    keys_out, ig_out, mg_out, m1_out, m2_out, nm_out, ng_out,
    kg_v, tab_v, w_v, m1_v, m2_v, mo_v, gl_v,
    u_all, ap, ao, w_o, w_p, ig_o, ig_p, pk_send, pk_recv, pk_own,
    gp, go, gp_send, gp_recv, go_send, go_recv, gz_send, gz_recv,
    dr_v, dr_low, dr_all, ds, ds_low, dz, base, mean_all, ga_low, gg, nm_v, ng_v, mg_v, m1o_v, m2o_v, keys_v,
    send_sem, recv_sem, local_sem, met,
):
    rep = lax.axis_index("rep")
    fsdp = lax.axis_index("fsdp")
    zl, y = rep // N_Y, rep % N_Y
    zh, x, core = fsdp // 8, (fsdp // 2) % N_X, fsdp % 2

    def chip_x(peer):
        return (rep, zh * 8 + peer * 2 + core)

    def chip_y(peer):
        return (zl * N_Y + peer, fsdp)

    def chip_zl(peer):
        return (peer * N_Y + y, fsdp)

    def at_y(step):
        return chip_y((y + step) % N_Y)

    def at_zl(step):
        return chip_zl((zl + step) % N_ZL)

    sibling = (rep, zh * 8 + x * 2 + (1 - core))
    partner = (rep, (1 - zh) * 8 + x * 2 + core)

    def remote(name, send, recv, src, dst, device):
        return pltpu.make_async_remote_copy(
            src_ref=src, dst_ref=dst, send_sem=send_sem.at[FIRST[name] + send],
            recv_sem=recv_sem.at[FIRST[name] + recv], device_id=device, device_id_type=MESH,
        )

    def local(name, src, dst):
        return pltpu.make_async_copy(src, dst, local_sem.at[LOCAL.index(name)])

    def signal(semaphore, device):
        pl.semaphore_signal(semaphore, inc=1, device_id=device, device_id_type=MESH)

    def wait_for(semaphore, count):
        @pl.when(count > 0)
        def _():
            pl.semaphore_wait(semaphore, count)

    own_rows = pl.ds(pl.multiple_of(core * ROWS, ROWS), ROWS)
    sib_rows = pl.ds(pl.multiple_of((1 - core) * ROWS, ROWS), ROWS)

    def columns(half, chip):
        return pl.ds(pl.multiple_of(half * (WIN // 2) + chip * COLS, COLS), COLS)

    def slot(chip):
        return pl.ds(pl.multiple_of(chip * TOK, TOK), TOK)

    barrier = pltpu.get_barrier_semaphore()
    for peer in range(1, N_X):
        @pl.when(peer > x)
        def _():
            signal(barrier, chip_x(peer))
    for peer in range(1, N_Y):
        @pl.when(peer > y)
        def _():
            signal(barrier, chip_y(peer))
    for peer in range(1, N_ZL):
        @pl.when(peer > zl)
        def _():
            signal(barrier, chip_zl(peer))

    @pl.when(core == 0)
    def _():
        signal(barrier, sibling)

    @pl.when(zh == 0)
    def _():
        signal(barrier, partner)

    loads = {
        "kg": local("kg", kg.at[0], kg_v),
        "tab": local("tab", tab.at[fsdp % 8], tab_v),
        "w": local("w", wt.at[0], w_v),
        "ap": local("ap", inp.at[0, :, columns(1 - zh, x)], ap.at[slot(x)]),
        "ao": local("ao", inp.at[0, :, columns(zh, x)], ao.at[slot(x)]),
        "dr": local("dr", dr, dr_v),
        "m1": local("m1", m1.at[0], m1_v),
        "m2": local("m2", m2.at[0], m2_v),
        "mo": local("mo", mo, mo_v),
        "gl": local("gl", gl, gl_v),
    }
    for copy in loads.values():
        copy.start()

    loads["kg"].wait()
    loads["tab"].wait()
    tables = (tab_v[0], tab_v[1])
    u_all[slot(x), :] = rotated_heads(kg_v[...].astype(F32), tables, -1.0).astype(BF16)
    loads["w"].wait()
    w_o[own_rows, :] = w_v[...].astype(BF16)

    loads["dr"].wait()
    for peer in range(N_Y):
        dr_low[peer] = dr_v[:, peer].reshape(N_ZL * 8, COLS).astype(BF16)

    wait_for(barrier, x + y + zl + core + zh)
    for peer in range(N_X - 1):
        @pl.when(peer < x)
        def _():
            signal(met.at[x], chip_x(peer))

    @pl.when(core == 1)
    def _():
        signal(met.at[MET_SIB], sibling)

    @pl.when(zh == 1)
    def _():
        signal(met.at[MET_Z], partner)

    for peer in range(N_Y - 1):
        @pl.when(peer < y)
        def _():
            signal(met.at[MET_Y], chip_y(peer))
    for peer in range(N_ZL - 1):
        @pl.when(peer < zl)
        def _():
            signal(met.at[MET_ZL], chip_zl(peer))

    wz = remote("wz", 0, 0, w_o.at[own_rows], w_p.at[own_rows], partner)
    wsib = remote("wsib", 0, 0, w_o.at[own_rows], w_o.at[own_rows], sibling)

    @pl.when(zh == 1)
    def _():
        wz.start()

    @pl.when(core == 1)
    def _():
        wsib.start()

    def to_x(name, src, dst):
        return [remote(name, peer, x, src(peer), dst(peer), chip_x(peer)) for peer in range(N_X)]

    def each_peer(act):
        for peer in range(N_X):
            pl.when(peer != x)(functools.partial(act, peer))

    def wait_x(name, shape_of):
        def wait(peer):
            remote(name, peer, peer, shape_of, shape_of, chip_x(peer)).wait_recv()

        each_peer(wait)

    tall = u_all.at[slot(0)]
    u_copy = to_x("u", lambda peer: u_all.at[slot(x)], lambda peer: u_all.at[slot(x)])
    ap_copy = to_x(
        "ap", lambda peer: inp.at[0, :, columns(1 - zh, peer)], lambda peer: ap.at[slot(x)]
    )
    ao_copy = to_x(
        "ao", lambda peer: inp.at[0, :, columns(zh, peer)], lambda peer: ao.at[slot(x)]
    )

    def first_sends(peer):
        @pl.when(peer > x)
        def _():
            pl.semaphore_wait(met.at[peer], 1)

        u_copy[peer].start()

    late = (zh == 1) & (core == 1)
    for peer in range(N_X - 1):
        pl.when(peer != x)(functools.partial(first_sends, peer))

    @pl.when((x != N_X - 1) & jnp.logical_not(late))
    def _():
        first_sends(N_X - 1)

    for peer in range(N_X):
        pl.when((peer != x) & ((peer < N_X - 1) | jnp.logical_not(late)))(ap_copy[peer].start)

    dy_copy = [
        remote("dy", e - 1, e - 1, dr_low.at[(y + e) % N_Y], dr_all.at[e - 1], at_y(e))
        for e in range(1, N_Y)
    ]
    wait_for(met.at[MET_Y], N_Y - 1 - y)
    for copy in dy_copy:
        copy.start()

    @pl.when((x != N_X - 1) & late)
    def _():
        first_sends(N_X - 1)
        ap_copy[N_X - 1].start()

    @pl.when(core == 0)
    def _():
        pl.semaphore_wait(met.at[MET_SIB], 1)
        wsib.start()

    each_peer(lambda peer: ao_copy[peer].start())

    @pl.when(zh == 0)
    def _():
        pl.semaphore_wait(met.at[MET_Z], 1)
        wz.start()

    wsib.wait_recv()
    wait_x("u", tall)
    ig_o[...] = lax.dot_general(
        u_all[...], w_o[...], (((1,), (1,)), ((), ())), preferred_element_type=F32
    ).astype(BF16)
    igo_copy = to_x(
        "igo", lambda peer: ig_o.at[slot(peer)], lambda peer: ig_out.at[0, :, columns(zh, x)]
    )
    each_peer(lambda peer: igo_copy[peer].start())
    outs = [local("igo", ig_o.at[slot(x)], ig_out.at[0, :, columns(zh, x)])]
    outs[0].start()

    for copy in dy_copy:
        copy.wait_recv()
    total = dr_v[:, y].reshape(N_ZL * 8, COLS)
    for e in range(N_Y - 1):
        total = total + dr_all[e].astype(F32)
    ds[...] = total
    ds_low[...] = total.astype(BF16)
    loads["mo"].wait()
    loads["gl"].wait()
    base[zl] = gl_v[...] - (outer_rate * outer_beta * outer_beta) * mo_v[...]
    dz_copy = [
        remote("dz", f - 1, f - 1, ds_low, dz.at[f - 1], at_zl(f)) for f in range(1, N_ZL)
    ]
    base_copy = [
        remote("base", f - 1, f - 1, base.at[zl], base.at[zl], at_zl(f)) for f in range(1, N_ZL)
    ]
    wait_for(met.at[MET_ZL], N_ZL - 1 - zl)
    for copy in dz_copy + base_copy:
        copy.start()

    loads["ap"].wait()
    wait_x("ap", tall)
    gp[...] = lax.dot_general(
        ap[...], u_all[...], (((0,), (0,)), ((), ())), preferred_element_type=F32
    )
    gp_send[...] = gp[sib_rows, :].astype(BF16)
    gpsib = remote("gpsib", 0, 0, gp_send, gp_recv, sibling)
    gpsib.start()

    wz.wait_recv()
    wfwd = remote("wfwd", 0, 0, w_p.at[own_rows], w_p.at[own_rows], sibling)
    wfwd.start()
    gpsib.wait_recv()
    gz_send[...] = (gp[own_rows, :] + gp_recv[...].astype(F32)).astype(BF16)
    wfwd.wait_recv()

    ig_p[...] = lax.dot_general(
        u_all[...], w_p[...], (((1,), (1,)), ((), ())), preferred_element_type=F32
    ).astype(BF16)
    igp_copy = to_x(
        "igp", lambda peer: ig_p.at[slot(peer)], lambda peer: ig_out.at[0, :, columns(1 - zh, x)]
    )
    each_peer(lambda peer: igp_copy[peer].start())
    outs.append(local("igp", ig_p.at[slot(x)], ig_out.at[0, :, columns(1 - zh, x)]))
    outs[-1].start()

    for copy in dz_copy + base_copy:
        copy.wait_recv()
    total = ds[...]
    for step in range(N_ZL - 1):
        total = total + dz[step].astype(F32)
    mean_all[...] = (total / N_REP).reshape(N_ZL, 8, COLS)
    fresh = base[...] - (outer_rate * (1.0 + outer_beta)) * mean_all[...]
    ga_low[...] = fresh.reshape(N_ZL * 8, COLS).astype(BF16)
    ay_copy = [remote("ay", e - 1, e - 1, ga_low, gg.at[y], at_y(e)) for e in range(1, N_Y)]
    for copy in ay_copy:
        copy.start()
    gg[y] = ga_low[...]
    mean_drift = mean_all[zl]
    moment = outer_beta * mo_v[...] + mean_drift
    nm_v[...] = moment
    ng_v[...] = gl_v[...] - outer_rate * (mean_drift + outer_beta * moment)
    outs.append(local("nm", nm_v, nm_out))
    outs[-1].start()
    outs.append(local("ng", ng_v, ng_out))
    outs[-1].start()

    gz = remote("gz", 0, 0, gz_send, gz_recv, partner)
    gz.start()

    loads["ao"].wait()
    wait_x("ao", tall)
    go[...] = lax.dot_general(
        ao[...], u_all[...], (((0,), (0,)), ((), ())), preferred_element_type=F32
    )
    go_send[...] = go[sib_rows, :].astype(BF16)
    gosib = remote("gosib", 0, 0, go_send, go_recv, sibling)
    gosib.start()

    pk_copy = to_x("pk", lambda peer: pk_send.at[peer], lambda peer: pk_recv.at[(peer - x + 3) % 4])
    for peer in range(N_X):
        part = jnp.dot(ao[slot(peer), :], w_o[...], preferred_element_type=F32)
        part += jnp.dot(ap[slot(peer), :], w_p[...], preferred_element_type=F32)

        @pl.when(peer == x)
        def _():
            pk_own[...] = part

        @pl.when(peer != x)
        def _():
            pk_send[peer] = part.astype(BF16)
            pk_copy[peer].start()

    loads["m1"].wait()
    loads["m2"].wait()
    gosib.wait_recv()
    for copy in ay_copy:
        copy.wait_recv()
    gz.wait_recv()

    for zone in range(N_ZL):
        rows = pl.ds(zone * 64, 64)
        gradient = (
            go[pl.ds(pl.multiple_of(core * ROWS + zone * 64, 64), 64), :]
            + go_recv[rows, :].astype(F32)
            + gz_recv[rows, :].astype(F32)
        )
        master = w_v[rows, :]
        spread = gg[:, pl.ds(zone * 8, 8), :].astype(F32).reshape(64, COLS)
        moment_one = beta_one * m1_v[rows, :].astype(F32) + (1.0 - beta_one) * gradient
        moment_two = (
            beta_two * m2_v[rows, :].astype(F32) + (1.0 - beta_two) * gradient * gradient
        )
        stepped = master - learning_rate * (
            moment_one / (jnp.sqrt(moment_two) + adam_epsilon) + weight_decay * master
        )
        mg_v[rows, :] = mixing * stepped + (1.0 - mixing) * spread
        m1o_v[rows, :] = moment_one.astype(BF16)
        m2o_v[rows, :] = moment_two.astype(BF16)
    for name, src, dst in (("mg", mg_v, mg_out), ("m1o", m1o_v, m1_out), ("m2o", m2o_v, m2_out)):
        outs.append(local(name, src, dst.at[0]))
        outs[-1].start()

    wait_x("pk", tall)
    projected = pk_own[...]
    for step in range(3):
        projected = projected + pk_recv[step].astype(F32)
    keys_v[...] = rotated_heads(projected, tables, 1.0).astype(BF16)
    outs.append(local("keys", keys_v, keys_out.at[0]))
    outs[-1].start()

    wait_x("igo", tall)
    wait_x("igp", tall)
    for copies in (u_copy, ap_copy, ao_copy, igo_copy, igp_copy, pk_copy):
        each_peer(lambda peer: copies[peer].wait_send())
    for copy in dy_copy + dz_copy + base_copy + ay_copy + [wz, wsib, wfwd, gpsib, gosib, gz]:
        copy.wait_send()
    for copy in outs:
        copy.wait()


PIECES = ((1, 32), (1, 32), (1, 32), (1, 32), (2, 128), (2, 128), (3, 256), (4, 256), (0, 128), (5, 8), (6, 8))


def hand_over(*refs):
    given, taken, held, sems = refs[:7], refs[7:14], refs[14:21], refs[21]
    loads, stores, done = [], [], [0] * 7
    for at, (which, rows) in enumerate(PIECES):
        src, dst = given[which], taken[which]
        if which < 5:
            src, dst = src.at[0], dst.at[0]
        part = pl.ds(done[which], rows)
        done[which] += rows
        loads.append(pltpu.make_async_copy(src.at[part], held[which].at[part], sems.at[0, at]))
        stores.append(pltpu.make_async_copy(held[which].at[part], dst.at[part], sems.at[1, at]))
    for copy in loads:
        copy.start()
    for load, store in zip(loads, stores):
        load.wait()
        store.start()
    for copy in stores:
        copy.wait()


def body(inputs, key_grads, weights, first_moment, second_moment, drift, momentum, global_weights):
    shape = jax.ShapeDtypeStruct
    vmem = pltpu.VMEM
    big = (4 * TOK, COLS)
    piece = (N_ZL, 8, COLS)
    scratch = [
        vmem((TOK, COLS), BF16), vmem((2, TOK, HEAD), F32), vmem((ROWS, COLS), F32),
        vmem((ROWS, COLS), BF16), vmem((ROWS, COLS), BF16), vmem((8, COLS), F32), vmem((8, COLS), F32),
        vmem(big, BF16), vmem(big, BF16), vmem(big, BF16), vmem(big, BF16), vmem(big, BF16),
        vmem(big, BF16), vmem(big, BF16),
        vmem((N_X, TOK, COLS), BF16), vmem((3, TOK, COLS), BF16), vmem((TOK, COLS), F32),
        vmem(big, F32), vmem(big, F32),
        vmem((ROWS, COLS), BF16), vmem((ROWS, COLS), BF16), vmem((ROWS, COLS), BF16),
        vmem((ROWS, COLS), BF16), vmem((ROWS, COLS), BF16), vmem((ROWS, COLS), BF16),
        vmem((N_ZL, N_Y, 8, COLS), F32), vmem((N_Y, N_ZL * 8, COLS), BF16), vmem((N_Y - 1, N_ZL * 8, COLS), BF16),
        vmem((N_ZL * 8, COLS), F32), vmem((N_ZL * 8, COLS), BF16),
        vmem((3, N_ZL * 8, COLS), BF16), vmem(piece, F32), vmem(piece, F32), vmem((N_ZL * 8, COLS), BF16),
        vmem((N_Y, N_ZL * 8, COLS), BF16), vmem((8, COLS), F32), vmem((8, COLS), F32), vmem((ROWS, COLS), F32),
        vmem((ROWS, COLS), BF16), vmem((ROWS, COLS), BF16), vmem((TOK, COLS), BF16),
        pltpu.SemaphoreType.DMA((N_REMOTE,)), pltpu.SemaphoreType.DMA((N_REMOTE,)),
        pltpu.SemaphoreType.DMA((len(LOCAL),)), pltpu.SemaphoreType.REGULAR((N_X + 4,)),
    ]
    outs = (
        shape((1, TOK, COLS), BF16), shape((1, TOK, WIN), BF16), shape((1, ROWS, COLS), F32),
        shape((1, ROWS, COLS), BF16), shape((1, ROWS, COLS), BF16),
        shape((8, COLS), F32), shape((8, COLS), F32),
    )
    anywhere = pl.BlockSpec(memory_space=pl.ANY)
    results = pl.pallas_call(
        kernel,
        out_shape=outs,
        in_specs=[anywhere] * 9,
        out_specs=[anywhere] * 7,
        scratch_shapes=scratch,
        compiler_params=pltpu.CompilerParams(
            collective_id=0, has_side_effects=True, vmem_limit_bytes=56 * 2**20
        ),
    )(
        inputs, key_grads, weights, first_moment, second_moment,
        drift.reshape(N_ZL, N_Y, 8, COLS), momentum, global_weights, jnp.asarray(rotary_tables()),
    )
    return pl.pallas_call(
        hand_over,
        out_shape=outs,
        in_specs=[anywhere] * 7,
        out_specs=[anywhere] * 7,
        scratch_shapes=[vmem(out.shape[-2:], out.dtype) for out in outs]
        + [pltpu.SemaphoreType.DMA((2, len(PIECES)))],
        compiler_params=pltpu.CompilerParams(vmem_limit_bytes=56 * 2**20),
    )(*results)


def solution(mesh):
    split = P("rep", "fsdp", None)
    rows = P(("fsdp", "rep"), None)
    return jax.shard_map(
        body,
        mesh=mesh,
        in_specs=(split,) * 6 + (rows,) * 2,
        out_specs=(split,) * 5 + (rows,) * 2,
        check_vma=False,
    )
```

```python
import functools

import jax
import jax.numpy as jnp
import numpy as np
from jax import lax
from jax.experimental import pallas as pl
from jax.experimental.pallas import tpu as pltpu
from jax.sharding import PartitionSpec as P

HEAD = 128
SEQ = 1024
TOK = 128
ROWS = 256
COLS = 512
WIN = 4096
N_REP = 32
N_X = 4
N_Y = 8
N_ZL = 4

learning_rate = 0.002
beta_one = 0.9
beta_two = 0.95
adam_epsilon = 1e-08
weight_decay = 0.1
outer_rate = 0.7
outer_beta = 0.9
mixing = 0.5
rope_base = 500000.0

F32 = jnp.float32
BF16 = jnp.bfloat16
MESH = pl.DeviceIdType.MESH


def rotary_tables():
    half = HEAD // 2
    freq = rope_base ** (-np.arange(half, dtype=np.float64) * (2.0 / HEAD))
    angles = np.arange(SEQ, dtype=np.float64)[:, None] * freq[None, :]
    cosine, sines = np.cos(angles), np.sin(angles)
    first = np.concatenate([cosine, cosine], axis=1)
    second = np.concatenate([-sines, sines], axis=1)
    both = np.stack([first, second]).astype(np.float32)
    return both.reshape(2, SEQ // TOK, TOK, HEAD).transpose(1, 0, 2, 3).copy()


def rotated_heads(values, tables, sign):
    cosine = tables[0]
    sines = sign * tables[1]
    heads = []
    for head in range(COLS // HEAD):
        part = values[:, head * HEAD : (head + 1) * HEAD]
        heads.append(part * cosine + pltpu.roll(part, HEAD // 2, 1) * sines)
    return jnp.concatenate(heads, axis=1)


REMOTE = (
    ("u", N_X), ("ap", N_X), ("ao", N_X), ("igo", N_X), ("igp", N_X), ("pk", N_X),
    ("wsib", 1), ("wz", 2), ("wfwd", 2), ("gpsib", 1), ("gosib", 1), ("gz", 1),
    ("dy", 7), ("dz", 3), ("ay", 7),
)
LOCAL = (
    "kg", "tab", "w", "m1", "m2", "mo", "gl", "ap", "ao", "dr",
    "igo", "igp", "mg", "m1o", "m2o", "nm", "ng", "keys",
)
FIRST = {}
N_REMOTE = 0
for _name, _count in REMOTE:
    FIRST[_name] = N_REMOTE
    N_REMOTE += _count
MET_SIB, MET_Z, MET_Y, MET_ZL = N_X, N_X + 1, N_X + 2, N_X + 3


def kernel(
    inp, kg, wt, m1, m2, dr, mo, gl, tab,
    keys_out, ig_out, mg_out, m1_out, m2_out, nm_out, ng_out,
    kg_v, tab_v, w_v, m1_v, m2_v, mo_v, gl_v,
    u_all, ap, ao, w_o, w_p, ig_o, ig_p, pk_send, pk_recv, pk_own,
    gp, go, gp_send, gp_recv, go_send, go_recv, gz_send, gz_recv,
    dr_v, dr_low, dr_all, ds, with_base, ds_low, dz, dz_wide, ga_low, gg, nm_v, ng_v, mg_v, m1o_v, m2o_v, keys_v,
    send_sem, recv_sem, local_sem, met,
):
    rep = lax.axis_index("rep")
    fsdp = lax.axis_index("fsdp")
    zl, y = rep // N_Y, rep % N_Y
    zh, x, core = fsdp // 8, (fsdp // 2) % N_X, fsdp % 2

    def chip_x(peer):
        return (rep, zh * 8 + peer * 2 + core)

    def chip_y(peer):
        return (zl * N_Y + peer, fsdp)

    def chip_zl(peer):
        return (peer * N_Y + y, fsdp)

    def at_y(step):
        return chip_y((y + step) % N_Y)

    def at_zl(step):
        return chip_zl((zl + step) % N_ZL)

    sibling = (rep, zh * 8 + x * 2 + (1 - core))
    partner = (rep, (1 - zh) * 8 + x * 2 + core)

    def remote(name, send, recv, src, dst, device):
        return pltpu.make_async_remote_copy(
            src_ref=src, dst_ref=dst, send_sem=send_sem.at[FIRST[name] + send],
            recv_sem=recv_sem.at[FIRST[name] + recv], device_id=device, device_id_type=MESH,
        )

    def local(name, src, dst):
        return pltpu.make_async_copy(src, dst, local_sem.at[LOCAL.index(name)])

    def signal(semaphore, device):
        pl.semaphore_signal(semaphore, inc=1, device_id=device, device_id_type=MESH)

    def wait_for(semaphore, count):
        @pl.when(count > 0)
        def _():
            pl.semaphore_wait(semaphore, count)

    own_rows = pl.ds(pl.multiple_of(core * ROWS, ROWS), ROWS)
    sib_rows = pl.ds(pl.multiple_of((1 - core) * ROWS, ROWS), ROWS)

    def columns(half, chip):
        return pl.ds(pl.multiple_of(half * (WIN // 2) + chip * COLS, COLS), COLS)

    def slot(chip):
        return pl.ds(pl.multiple_of(chip * TOK, TOK), TOK)

    barrier = pltpu.get_barrier_semaphore()
    for peer in range(1, N_X):
        @pl.when(peer > x)
        def _():
            signal(barrier, chip_x(peer))
    for peer in range(1, N_Y):
        @pl.when(peer > y)
        def _():
            signal(barrier, chip_y(peer))
    for peer in range(1, N_ZL):
        @pl.when(peer > zl)
        def _():
            signal(barrier, chip_zl(peer))

    @pl.when(core == 0)
    def _():
        signal(barrier, sibling)

    @pl.when(zh == 0)
    def _():
        signal(barrier, partner)

    loads = {
        "kg": local("kg", kg.at[0], kg_v),
        "tab": local("tab", tab.at[fsdp % 8], tab_v),
        "w": local("w", wt.at[0], w_v),
        "ap": local("ap", inp.at[0, :, columns(1 - zh, x)], ap.at[slot(x)]),
        "ao": local("ao", inp.at[0, :, columns(zh, x)], ao.at[slot(x)]),
        "dr": local("dr", dr, dr_v),
        "m1": local("m1", m1.at[0], m1_v),
        "m2": local("m2", m2.at[0], m2_v),
        "mo": local("mo", mo, mo_v),
        "gl": local("gl", gl, gl_v),
    }
    for copy in loads.values():
        copy.start()

    loads["kg"].wait()
    loads["tab"].wait()
    tables = (tab_v[0], tab_v[1])
    u_all[slot(x), :] = rotated_heads(kg_v[...].astype(F32), tables, -1.0).astype(BF16)
    loads["w"].wait()
    w_o[own_rows, :] = w_v[...].astype(BF16)

    loads["dr"].wait()
    for peer in range(N_Y):
        dr_low[peer] = dr_v[:, peer].reshape(N_ZL * 8, COLS).astype(BF16)

    wait_for(barrier, x + y + zl + core + zh)
    for peer in range(N_X - 1):
        @pl.when(peer < x)
        def _():
            signal(met.at[x], chip_x(peer))

    @pl.when(core == 1)
    def _():
        signal(met.at[MET_SIB], sibling)

    @pl.when(zh == 1)
    def _():
        signal(met.at[MET_Z], partner)

    for peer in range(N_Y - 1):
        @pl.when(peer < y)
        def _():
            signal(met.at[MET_Y], chip_y(peer))
    for peer in range(N_ZL - 1):
        @pl.when(peer < zl)
        def _():
            signal(met.at[MET_ZL], chip_zl(peer))

    def half_rows(half):
        return pl.ds(pl.multiple_of(core * ROWS + half * (ROWS // 2), ROWS // 2), ROWS // 2)

    wz = [
        remote("wz", half, half, w_o.at[half_rows(half)], w_p.at[half_rows(half)], partner)
        for half in range(2)
    ]
    wsib = remote("wsib", 0, 0, w_o.at[own_rows], w_o.at[own_rows], sibling)

    @pl.when(zh == 1)
    def _():
        wz[0].start()
        wz[1].start()

    @pl.when(core == 1)
    def _():
        wsib.start()

    def to_x(name, src, dst):
        return [remote(name, peer, x, src(peer), dst(peer), chip_x(peer)) for peer in range(N_X)]

    def each_peer(act):
        for peer in range(N_X):
            pl.when(peer != x)(functools.partial(act, peer))

    def wait_x(name, shape_of):
        def wait(peer):
            remote(name, peer, peer, shape_of, shape_of, chip_x(peer)).wait_recv()

        each_peer(wait)

    tall = u_all.at[slot(0)]
    u_copy = to_x("u", lambda peer: u_all.at[slot(x)], lambda peer: u_all.at[slot(x)])
    ap_copy = to_x(
        "ap", lambda peer: inp.at[0, :, columns(1 - zh, peer)], lambda peer: ap.at[slot(x)]
    )
    ao_copy = to_x(
        "ao", lambda peer: inp.at[0, :, columns(zh, peer)], lambda peer: ao.at[slot(x)]
    )

    def first_sends(peer):
        @pl.when(peer > x)
        def _():
            pl.semaphore_wait(met.at[peer], 1)

        u_copy[peer].start()

    late = (zh == 1) & (core == 1)
    for peer in range(N_X - 1):
        pl.when(peer != x)(functools.partial(first_sends, peer))

    @pl.when((x != N_X - 1) & jnp.logical_not(late))
    def _():
        first_sends(N_X - 1)

    for peer in range(N_X):
        pl.when((peer != x) & ((peer < N_X - 1) | jnp.logical_not(late)))(ap_copy[peer].start)

    dy_copy = [
        remote("dy", e - 1, e - 1, dr_low.at[(y + e) % N_Y], dr_all.at[e - 1], at_y(e))
        for e in range(1, N_Y)
    ]
    wait_for(met.at[MET_Y], N_Y - 1 - y)
    for copy in dy_copy:
        copy.start()

    @pl.when((x != N_X - 1) & late)
    def _():
        first_sends(N_X - 1)
        ap_copy[N_X - 1].start()

    @pl.when(core == 0)
    def _():
        pl.semaphore_wait(met.at[MET_SIB], 1)
        wsib.start()

    each_peer(lambda peer: ao_copy[peer].start())

    @pl.when(zh == 0)
    def _():
        pl.semaphore_wait(met.at[MET_Z], 1)
        wz[0].start()
        wz[1].start()

    wsib.wait_recv()
    wait_x("u", tall)
    ig_o[...] = lax.dot_general(
        u_all[...], w_o[...], (((1,), (1,)), ((), ())), preferred_element_type=F32
    ).astype(BF16)
    igo_copy = to_x(
        "igo", lambda peer: ig_o.at[slot(peer)], lambda peer: ig_out.at[0, :, columns(zh, x)]
    )
    each_peer(lambda peer: igo_copy[peer].start())
    outs = [local("igo", ig_o.at[slot(x)], ig_out.at[0, :, columns(zh, x)])]
    outs[0].start()

    for copy in dy_copy:
        copy.wait_recv()
    total = dr_v[:, y].reshape(N_ZL * 8, COLS)
    for e in range(N_Y - 1):
        total = total + dr_all[e].astype(F32)
    ds[...] = total.reshape(N_ZL, 8, COLS)
    loads["mo"].wait()
    loads["gl"].wait()
    with_base[...] = ds[...]
    base = gl_v[...] - (outer_rate * outer_beta * outer_beta) * mo_v[...]
    with_base[zl] = ds[zl] - (N_REP / (outer_rate * (1.0 + outer_beta))) * base
    ds_low[...] = with_base[...].reshape(N_ZL * 8, COLS).astype(BF16)
    dz_copy = [
        remote("dz", f - 1, f - 1, ds_low, dz.at[f - 1], at_zl(f)) for f in range(1, N_ZL)
    ]
    wait_for(met.at[MET_ZL], N_ZL - 1 - zl)
    for copy in dz_copy:
        copy.start()

    loads["ap"].wait()
    wait_x("ap", tall)
    gp[...] = lax.dot_general(
        ap[...], u_all[...], (((0,), (0,)), ((), ())), preferred_element_type=F32
    )
    gp_send[...] = gp[sib_rows, :].astype(BF16)
    gpsib = remote("gpsib", 0, 0, gp_send, gp_recv, sibling)
    gpsib.start()

    gpsib.wait_recv()
    gz_send[...] = (gp[own_rows, :] + gp_recv[...].astype(F32)).astype(BF16)
    gz = remote("gz", 0, 0, gz_send, gz_recv, partner)

    @pl.when(zh == 1)
    def _():
        gz.start()

    wfwd = [
        remote("wfwd", half, half, w_p.at[half_rows(half)], w_p.at[half_rows(half)], sibling)
        for half in range(2)
    ]
    for half in range(2):
        wz[half].wait_recv()
        wfwd[half].start()
    for copy in wfwd:
        copy.wait_recv()

    ig_p[...] = lax.dot_general(
        u_all[...], w_p[...], (((1,), (1,)), ((), ())), preferred_element_type=F32
    ).astype(BF16)
    igp_copy = to_x(
        "igp", lambda peer: ig_p.at[slot(peer)], lambda peer: ig_out.at[0, :, columns(1 - zh, x)]
    )
    each_peer(lambda peer: igp_copy[peer].start())
    outs.append(local("igp", ig_p.at[slot(x)], ig_out.at[0, :, columns(1 - zh, x)]))
    outs[-1].start()

    loads["ao"].wait()
    wait_x("ao", tall)
    go[...] = lax.dot_general(
        ao[...], u_all[...], (((0,), (0,)), ((), ())), preferred_element_type=F32
    )
    go_send[...] = go[sib_rows, :].astype(BF16)
    gosib = remote("gosib", 0, 0, go_send, go_recv, sibling)
    gosib.start()

    pk_copy = to_x("pk", lambda peer: pk_send.at[peer], lambda peer: pk_recv.at[(peer - x + 3) % 4])
    for peer in range(N_X):
        part = jnp.dot(ao[slot(peer), :], w_o[...], preferred_element_type=F32)
        part += jnp.dot(ap[slot(peer), :], w_p[...], preferred_element_type=F32)

        @pl.when(peer == x)
        def _():
            pk_own[...] = part

        @pl.when(peer != x)
        def _():
            pk_send[peer] = part.astype(BF16)
            pk_copy[peer].start()

    @pl.when(zh == 0)
    def _():
        gz.start()

    for copy in dz_copy:
        copy.wait_recv()
    total = with_base[...].reshape(N_ZL * 8, COLS)
    for step in range(N_ZL - 1):
        total = total + dz[step].astype(F32)
    ga_low[...] = ((-outer_rate * (1.0 + outer_beta) / N_REP) * total).astype(BF16)
    ay_copy = [remote("ay", e - 1, e - 1, ga_low, gg.at[y], at_y(e)) for e in range(1, N_Y)]
    for copy in ay_copy:
        copy.start()
    gg[y] = ga_low[...]
    own_piece = pl.ds(pl.multiple_of(zl * 8, 8), 8)
    own_total = ds[zl]
    for step in range(N_ZL - 1):
        dz_wide[step] = dz[step].astype(F32)
        own_total = own_total + dz_wide[step, own_piece, :]
    mean_drift = own_total / N_REP
    moment = outer_beta * mo_v[...] + mean_drift
    nm_v[...] = moment
    ng_v[...] = gl_v[...] - outer_rate * (mean_drift + outer_beta * moment)
    outs.append(local("nm", nm_v, nm_out))
    outs[-1].start()
    outs.append(local("ng", ng_v, ng_out))
    outs[-1].start()

    loads["m1"].wait()
    loads["m2"].wait()
    gosib.wait_recv()
    for copy in ay_copy:
        copy.wait_recv()
    gz.wait_recv()

    for zone in range(N_ZL):
        rows = pl.ds(zone * 64, 64)
        gradient = (
            go[pl.ds(pl.multiple_of(core * ROWS + zone * 64, 64), 64), :]
            + go_recv[rows, :].astype(F32)
            + gz_recv[rows, :].astype(F32)
        )
        master = w_v[rows, :]
        spread = gg[:, pl.ds(zone * 8, 8), :].astype(F32).reshape(64, COLS)
        moment_one = beta_one * m1_v[rows, :].astype(F32) + (1.0 - beta_one) * gradient
        moment_two = (
            beta_two * m2_v[rows, :].astype(F32) + (1.0 - beta_two) * gradient * gradient
        )
        stepped = master - learning_rate * (
            moment_one / (jnp.sqrt(moment_two) + adam_epsilon) + weight_decay * master
        )
        mg_v[rows, :] = mixing * stepped + (1.0 - mixing) * spread
        m1o_v[rows, :] = moment_one.astype(BF16)
        m2o_v[rows, :] = moment_two.astype(BF16)
    for name, src, dst in (("mg", mg_v, mg_out), ("m1o", m1o_v, m1_out), ("m2o", m2o_v, m2_out)):
        outs.append(local(name, src, dst.at[0]))
        outs[-1].start()

    wait_x("pk", tall)
    projected = pk_own[...]
    for step in range(3):
        projected = projected + pk_recv[step].astype(F32)
    keys_v[...] = rotated_heads(projected, tables, 1.0).astype(BF16)
    outs.append(local("keys", keys_v, keys_out.at[0]))
    outs[-1].start()

    wait_x("igo", tall)
    wait_x("igp", tall)
    for copies in (u_copy, ap_copy, ao_copy, igo_copy, igp_copy, pk_copy):
        each_peer(lambda peer: copies[peer].wait_send())
    for copy in dy_copy + dz_copy + ay_copy + wz + wfwd + [wsib, gpsib, gosib, gz]:
        copy.wait_send()
    for copy in outs:
        copy.wait()


def hand_over(*refs):
    given, taken, sems = refs[:7], refs[7:14], refs[14]
    copies = [
        pltpu.make_async_copy(src, dst, sems.at[at])
        for at, (src, dst) in enumerate(zip(given, taken))
    ]
    for copy in copies:
        copy.start()
    for copy in copies:
        copy.wait()


def body(inputs, key_grads, weights, first_moment, second_moment, drift, momentum, global_weights):
    shape = jax.ShapeDtypeStruct
    vmem = pltpu.VMEM
    big = (4 * TOK, COLS)
    piece = (N_ZL, 8, COLS)
    scratch = [
        vmem((TOK, COLS), BF16), vmem((2, TOK, HEAD), F32), vmem((ROWS, COLS), F32),
        vmem((ROWS, COLS), BF16), vmem((ROWS, COLS), BF16), vmem((8, COLS), F32), vmem((8, COLS), F32),
        vmem(big, BF16), vmem(big, BF16), vmem(big, BF16), vmem(big, BF16), vmem(big, BF16),
        vmem(big, BF16), vmem(big, BF16),
        vmem((N_X, TOK, COLS), BF16), vmem((3, TOK, COLS), BF16), vmem((TOK, COLS), F32),
        vmem(big, F32), vmem(big, F32),
        vmem((ROWS, COLS), BF16), vmem((ROWS, COLS), BF16), vmem((ROWS, COLS), BF16),
        vmem((ROWS, COLS), BF16), vmem((ROWS, COLS), BF16), vmem((ROWS, COLS), BF16),
        vmem((N_ZL, N_Y, 8, COLS), F32), vmem((N_Y, N_ZL * 8, COLS), BF16), vmem((N_Y - 1, N_ZL * 8, COLS), BF16),
        vmem(piece, F32), vmem(piece, F32), vmem((N_ZL * 8, COLS), BF16),
        vmem((3, N_ZL * 8, COLS), BF16), vmem((3, N_ZL * 8, COLS), F32), vmem((N_ZL * 8, COLS), BF16),
        vmem((N_Y, N_ZL * 8, COLS), BF16), vmem((8, COLS), F32), vmem((8, COLS), F32), vmem((ROWS, COLS), F32),
        vmem((ROWS, COLS), BF16), vmem((ROWS, COLS), BF16), vmem((TOK, COLS), BF16),
        pltpu.SemaphoreType.DMA((N_REMOTE,)), pltpu.SemaphoreType.DMA((N_REMOTE,)),
        pltpu.SemaphoreType.DMA((len(LOCAL),)), pltpu.SemaphoreType.REGULAR((N_X + 4,)),
    ]
    outs = (
        shape((1, TOK, COLS), BF16), shape((1, TOK, WIN), BF16), shape((1, ROWS, COLS), F32),
        shape((1, ROWS, COLS), BF16), shape((1, ROWS, COLS), BF16),
        shape((8, COLS), F32), shape((8, COLS), F32),
    )
    anywhere = pl.BlockSpec(memory_space=pl.ANY)
    results = pl.pallas_call(
        kernel,
        out_shape=tuple(vmem(out.shape, out.dtype) for out in outs),
        in_specs=[anywhere] * 9,
        out_specs=[anywhere] * 7,
        scratch_shapes=scratch,
        compiler_params=pltpu.CompilerParams(
            collective_id=0, has_side_effects=True, vmem_limit_bytes=56 * 2**20
        ),
    )(
        inputs, key_grads, weights, first_moment, second_moment,
        drift.reshape(N_ZL, N_Y, 8, COLS), momentum, global_weights, jnp.asarray(rotary_tables()),
    )
    return pl.pallas_call(
        hand_over,
        out_shape=outs,
        in_specs=[anywhere] * 7,
        out_specs=[anywhere] * 7,
        scratch_shapes=[pltpu.SemaphoreType.DMA((7,))],
        compiler_params=pltpu.CompilerParams(vmem_limit_bytes=56 * 2**20),
    )(*[pltpu.with_memory_space_constraint(result, pltpu.VMEM) for result in results])


def solution(mesh):
    split = P("rep", "fsdp", None)
    rows = P(("fsdp", "rep"), None)
    return jax.shard_map(
        body,
        mesh=mesh,
        in_specs=(split,) * 6 + (rows,) * 2,
        out_specs=(split,) * 5 + (rows,) * 2,
        check_vma=False,
    )
```

```python
import functools

import jax
import jax.numpy as jnp
import numpy as np
from jax import lax
from jax.experimental import pallas as pl
from jax.experimental.pallas import tpu as pltpu
from jax.sharding import PartitionSpec as P

HEAD = 128
SEQ = 1024
TOK = 128
ROWS = 256
COLS = 512
WIN = 4096
N_REP = 32
N_X = 4
N_Y = 8
N_ZL = 4

learning_rate = 0.002
beta_one = 0.9
beta_two = 0.95
adam_epsilon = 1e-08
weight_decay = 0.1
outer_rate = 0.7
outer_beta = 0.9
mixing = 0.5
rope_base = 500000.0

F32 = jnp.float32
BF16 = jnp.bfloat16
MESH = pl.DeviceIdType.MESH


def rotary_tables():
    half = HEAD // 2
    freq = rope_base ** (-np.arange(half, dtype=np.float64) * (2.0 / HEAD))
    angles = np.arange(SEQ, dtype=np.float64)[:, None] * freq[None, :]
    cosine, sines = np.cos(angles), np.sin(angles)
    first = np.concatenate([cosine, cosine], axis=1)
    second = np.concatenate([-sines, sines], axis=1)
    both = np.stack([first, second]).astype(np.float32)
    return both.reshape(2, SEQ // TOK, TOK, HEAD).transpose(1, 0, 2, 3).copy()


def rotated_heads(values, tables, sign):
    cosine = tables[0]
    sines = sign * tables[1]
    heads = []
    for head in range(COLS // HEAD):
        part = values[:, head * HEAD : (head + 1) * HEAD]
        heads.append(part * cosine + pltpu.roll(part, HEAD // 2, 1) * sines)
    return jnp.concatenate(heads, axis=1)


REMOTE = (
    ("u", N_X), ("ap", N_X), ("ao", N_X), ("igo", N_X), ("igp", N_X), ("pk", N_X),
    ("wsib", 1), ("wz", 2), ("wfwd", 2), ("gpsib", 1), ("gosib", 1), ("gz", 1),
    ("dy", 7), ("dz", 3), ("ay", 7),
)
LOCAL = (
    "kg", "tab", "w", "m1", "m2", "mo", "gl", "ap", "ao", "dr",
    "igo", "igp", "mg", "m1o", "m2o", "nm", "ng", "keys",
)
FIRST = {}
N_REMOTE = 0
for _name, _count in REMOTE:
    FIRST[_name] = N_REMOTE
    N_REMOTE += _count
MET_Z, MET_Y, MET_ZL = 0, 1, 2
FAR_FIRST = (4, 3, 5, 2, 6, 1, 7)


def kernel(
    inp, kg, wt, m1, m2, dr, mo, gl, tab,
    keys_out, ig_out, mg_out, m1_out, m2_out, nm_out, ng_out,
    kg_v, tab_v, w_v, m1_v, m2_v, mo_v, gl_v,
    u_all, ap, ao, w_o, w_p, ig_o, ig_p, pk_send, pk_recv, pk_own,
    gp, go, gp_send, gp_recv, go_send, go_recv, gz_send, gz_recv,
    dr_v, dr_low, dr_all, ds, with_base, ds_low, dz, dz_wide, ga_low, gg, nm_v, ng_v, mg_v, m1o_v, m2o_v, keys_v,
    send_sem, recv_sem, local_sem, met,
):
    rep = lax.axis_index("rep")
    fsdp = lax.axis_index("fsdp")
    zl, y = rep // N_Y, rep % N_Y
    zh, x, core = fsdp // 8, (fsdp // 2) % N_X, fsdp % 2

    def chip_x(peer):
        return (rep, zh * 8 + peer * 2 + core)

    def chip_y(peer):
        return (zl * N_Y + peer, fsdp)

    def chip_zl(peer):
        return (peer * N_Y + y, fsdp)

    def at_y(step):
        return chip_y((y + step) % N_Y)

    def at_zl(step):
        return chip_zl((zl + step) % N_ZL)

    sibling = (rep, zh * 8 + x * 2 + (1 - core))
    partner = (rep, (1 - zh) * 8 + x * 2 + core)

    def remote(name, send, recv, src, dst, device):
        return pltpu.make_async_remote_copy(
            src_ref=src, dst_ref=dst, send_sem=send_sem.at[FIRST[name] + send],
            recv_sem=recv_sem.at[FIRST[name] + recv], device_id=device, device_id_type=MESH,
        )

    def local(name, src, dst):
        return pltpu.make_async_copy(src, dst, local_sem.at[LOCAL.index(name)])

    def signal(semaphore, device):
        pl.semaphore_signal(semaphore, inc=1, device_id=device, device_id_type=MESH)

    def wait_for(semaphore, count):
        @pl.when(count > 0)
        def _():
            pl.semaphore_wait(semaphore, count)

    own_rows = pl.ds(pl.multiple_of(core * ROWS, ROWS), ROWS)
    sib_rows = pl.ds(pl.multiple_of((1 - core) * ROWS, ROWS), ROWS)

    def columns(half, chip):
        return pl.ds(pl.multiple_of(half * (WIN // 2) + chip * COLS, COLS), COLS)

    def slot(chip):
        return pl.ds(pl.multiple_of(chip * TOK, TOK), TOK)

    barrier = pltpu.get_barrier_semaphore()
    for step in range(1, N_X):
        signal(barrier, chip_x((x + step) % N_X))
    signal(barrier, sibling)
    for peer in range(1, N_Y):
        @pl.when(peer > y)
        def _():
            signal(barrier, chip_y(peer))
    for peer in range(1, N_ZL):
        @pl.when(peer > zl)
        def _():
            signal(barrier, chip_zl(peer))

    @pl.when(zh == 0)
    def _():
        signal(barrier, partner)

    loads = {
        "kg": local("kg", kg.at[0], kg_v),
        "tab": local("tab", tab.at[fsdp % 8], tab_v),
        "w": local("w", wt.at[0], w_v),
        "ap": local("ap", inp.at[0, :, columns(1 - zh, x)], ap.at[slot(x)]),
        "ao": local("ao", inp.at[0, :, columns(zh, x)], ao.at[slot(x)]),
        "dr": local("dr", dr, dr_v),
        "m1": local("m1", m1.at[0], m1_v),
        "m2": local("m2", m2.at[0], m2_v),
        "mo": local("mo", mo, mo_v),
        "gl": local("gl", gl, gl_v),
    }
    for name in ("kg", "tab", "w", "dr"):
        loads[name].start()

    pl.semaphore_wait(barrier, N_X + y + zl + zh)

    @pl.when(zh == 1)
    def _():
        signal(met.at[MET_Z], partner)

    for peer in range(N_Y - 1):
        @pl.when(peer < y)
        def _():
            signal(met.at[MET_Y], chip_y(peer))
    for peer in range(N_ZL - 1):
        @pl.when(peer < zl)
        def _():
            signal(met.at[MET_ZL], chip_zl(peer))

    for name in ("ap", "ao", "m1", "m2", "mo", "gl"):
        loads[name].start()

    loads["kg"].wait()
    loads["tab"].wait()
    tables = (tab_v[0], tab_v[1])
    u_all[slot(x), :] = rotated_heads(kg_v[...].astype(F32), tables, -1.0).astype(BF16)
    loads["w"].wait()
    w_o[own_rows, :] = w_v[...].astype(BF16)

    loads["dr"].wait()
    for peer in range(N_Y):
        dr_low[peer] = dr_v[:, peer].reshape(N_ZL * 8, COLS).astype(BF16)

    ahead = zl < N_ZL // 2
    behind = jnp.logical_not(ahead)

    def half_rows(half):
        return pl.ds(pl.multiple_of(core * ROWS + half * (ROWS // 2), ROWS // 2), ROWS // 2)

    wz = [
        remote("wz", half, half, w_o.at[half_rows(half)], w_p.at[half_rows(half)], partner)
        for half in range(2)
    ]
    wsib = remote("wsib", 0, 0, w_o.at[own_rows], w_o.at[own_rows], sibling)

    @pl.when(zh == 1)
    def _():
        wz[0].start()
        wz[1].start()

    wsib.start()

    def to_x(name, src, dst):
        return [remote(name, peer, x, src(peer), dst(peer), chip_x(peer)) for peer in range(N_X)]

    def each_peer(act):
        for peer in range(N_X):
            pl.when(peer != x)(functools.partial(act, peer))

    def wait_x(name, shape_of):
        def wait(peer):
            remote(name, peer, peer, shape_of, shape_of, chip_x(peer)).wait_recv()

        each_peer(wait)

    tall = u_all.at[slot(0)]
    u_copy = to_x("u", lambda peer: u_all.at[slot(x)], lambda peer: u_all.at[slot(x)])
    ap_copy = to_x(
        "ap", lambda peer: inp.at[0, :, columns(1 - zh, peer)], lambda peer: ap.at[slot(x)]
    )
    ao_copy = to_x(
        "ao", lambda peer: inp.at[0, :, columns(zh, peer)], lambda peer: ao.at[slot(x)]
    )

    each_peer(lambda peer: u_copy[peer].start())
    each_peer(lambda peer: ap_copy[peer].start())

    dy_copy = [
        remote("dy", e - 1, e - 1, dr_low.at[(y + e) % N_Y], dr_all.at[e - 1], at_y(e))
        for e in range(1, N_Y)
    ]
    wait_for(met.at[MET_Y], N_Y - 1 - y)
    for e in FAR_FIRST:
        dy_copy[e - 1].start()

    each_peer(lambda peer: ao_copy[peer].start())

    @pl.when(zh == 0)
    def _():
        pl.semaphore_wait(met.at[MET_Z], 1)
        wz[0].start()
        wz[1].start()

    wsib.wait_recv()
    wait_x("u", tall)
    ig_o[...] = lax.dot_general(
        u_all[...], w_o[...], (((1,), (1,)), ((), ())), preferred_element_type=F32
    ).astype(BF16)
    igo_copy = to_x(
        "igo", lambda peer: ig_o.at[slot(peer)], lambda peer: ig_out.at[0, :, columns(zh, x)]
    )
    each_peer(lambda peer: igo_copy[peer].start())
    outs = [local("igo", ig_o.at[slot(x)], ig_out.at[0, :, columns(zh, x)])]
    outs[0].start()

    for copy in dy_copy:
        copy.wait_recv()
    total = dr_v[:, y].reshape(N_ZL * 8, COLS)
    for e in range(N_Y - 1):
        total = total + dr_all[e].astype(F32)
    ds[...] = total.reshape(N_ZL, 8, COLS)
    loads["mo"].wait()
    loads["gl"].wait()
    with_base[...] = ds[...]
    base = gl_v[...] - (outer_rate * outer_beta * outer_beta) * mo_v[...]
    with_base[zl] = ds[zl] - (N_REP / (outer_rate * (1.0 + outer_beta))) * base
    ds_low[...] = with_base[...].reshape(N_ZL * 8, COLS).astype(BF16)
    dz_copy = [
        remote("dz", f - 1, f - 1, ds_low, dz.at[f - 1], at_zl(f)) for f in range(1, N_ZL)
    ]
    wait_for(met.at[MET_ZL], N_ZL - 1 - zl)
    for copy in dz_copy:
        copy.start()

    loads["ap"].wait()
    wait_x("ap", tall)
    gp[...] = lax.dot_general(
        ap[...], u_all[...], (((0,), (0,)), ((), ())), preferred_element_type=F32
    )
    gp_send[...] = gp[sib_rows, :].astype(BF16)
    gpsib = remote("gpsib", 0, 0, gp_send, gp_recv, sibling)
    gpsib.start()

    gpsib.wait_recv()
    gz_send[...] = (gp[own_rows, :] + gp_recv[...].astype(F32)).astype(BF16)
    gz = remote("gz", 0, 0, gz_send, gz_recv, partner)

    @pl.when(zh == 1)
    def _():
        gz.start()

    wfwd = [
        remote("wfwd", half, half, w_p.at[half_rows(half)], w_p.at[half_rows(half)], sibling)
        for half in range(2)
    ]
    for half in range(2):
        wz[half].wait_recv()
        wfwd[half].start()
    for copy in wfwd:
        copy.wait_recv()

    ig_p[...] = lax.dot_general(
        u_all[...], w_p[...], (((1,), (1,)), ((), ())), preferred_element_type=F32
    ).astype(BF16)
    igp_copy = to_x(
        "igp", lambda peer: ig_p.at[slot(peer)], lambda peer: ig_out.at[0, :, columns(1 - zh, x)]
    )
    each_peer(lambda peer: igp_copy[peer].start())
    outs.append(local("igp", ig_p.at[slot(x)], ig_out.at[0, :, columns(1 - zh, x)]))
    outs[-1].start()

    loads["ao"].wait()
    wait_x("ao", tall)
    go[...] = lax.dot_general(
        ao[...], u_all[...], (((0,), (0,)), ((), ())), preferred_element_type=F32
    )
    go_send[...] = go[sib_rows, :].astype(BF16)
    gosib = remote("gosib", 0, 0, go_send, go_recv, sibling)
    gosib.start()

    pk_copy = to_x("pk", lambda peer: pk_send.at[peer], lambda peer: pk_recv.at[(peer - x + 3) % 4])
    for peer in range(N_X):
        part = jnp.dot(ao[slot(peer), :], w_o[...], preferred_element_type=F32)
        part += jnp.dot(ap[slot(peer), :], w_p[...], preferred_element_type=F32)

        @pl.when(peer == x)
        def _():
            pk_own[...] = part

        @pl.when(peer != x)
        def _():
            pk_send[peer] = part.astype(BF16)
            pk_copy[peer].start()

    @pl.when(zh == 0)
    def _():
        gz.start()

    for copy in dz_copy:
        copy.wait_recv()
    total = with_base[...].reshape(N_ZL * 8, COLS)
    for step in range(N_ZL - 1):
        total = total + dz[step].astype(F32)
    ga_low[...] = ((-outer_rate * (1.0 + outer_beta) / N_REP) * total).astype(BF16)
    ay_copy = [remote("ay", e - 1, e - 1, ga_low, gg.at[y], at_y(e)) for e in range(1, N_Y)]
    for e in FAR_FIRST:
        ay_copy[e - 1].start()
    gg[y] = ga_low[...]
    own_piece = pl.ds(pl.multiple_of(zl * 8, 8), 8)
    own_total = ds[zl]
    for step in range(N_ZL - 1):
        dz_wide[step] = dz[step].astype(F32)
        own_total = own_total + dz_wide[step, own_piece, :]
    mean_drift = own_total / N_REP
    moment = outer_beta * mo_v[...] + mean_drift
    nm_v[...] = moment
    ng_v[...] = gl_v[...] - outer_rate * (mean_drift + outer_beta * moment)
    outs.append(local("nm", nm_v, nm_out))
    outs[-1].start()
    outs.append(local("ng", ng_v, ng_out))
    outs[-1].start()

    loads["m1"].wait()
    loads["m2"].wait()
    gosib.wait_recv()
    for copy in ay_copy:
        copy.wait_recv()
    gz.wait_recv()

    for zone in range(N_ZL):
        rows = pl.ds(zone * 64, 64)
        gradient = (
            go[pl.ds(pl.multiple_of(core * ROWS + zone * 64, 64), 64), :]
            + go_recv[rows, :].astype(F32)
            + gz_recv[rows, :].astype(F32)
        )
        master = w_v[rows, :]
        spread = gg[:, pl.ds(zone * 8, 8), :].astype(F32).reshape(64, COLS)
        moment_one = beta_one * m1_v[rows, :].astype(F32) + (1.0 - beta_one) * gradient
        moment_two = (
            beta_two * m2_v[rows, :].astype(F32) + (1.0 - beta_two) * gradient * gradient
        )
        stepped = master - learning_rate * (
            moment_one / (jnp.sqrt(moment_two) + adam_epsilon) + weight_decay * master
        )
        mg_v[rows, :] = mixing * stepped + (1.0 - mixing) * spread
        m1o_v[rows, :] = moment_one.astype(BF16)
        m2o_v[rows, :] = moment_two.astype(BF16)
    for name, src, dst in (("mg", mg_v, mg_out), ("m1o", m1o_v, m1_out), ("m2o", m2o_v, m2_out)):
        outs.append(local(name, src, dst.at[0]))
        outs[-1].start()

    wait_x("pk", tall)
    projected = pk_own[...]
    for step in range(3):
        projected = projected + pk_recv[step].astype(F32)
    keys_v[...] = rotated_heads(projected, tables, 1.0).astype(BF16)
    outs.append(local("keys", keys_v, keys_out.at[0]))
    outs[-1].start()

    wait_x("igo", tall)
    wait_x("igp", tall)
    for copies in (u_copy, ap_copy, ao_copy, igo_copy, igp_copy, pk_copy):
        each_peer(lambda peer: copies[peer].wait_send())
    for copy in dy_copy + dz_copy + ay_copy + wz + wfwd + [wsib, gpsib, gosib, gz]:
        copy.wait_send()
    for copy in outs:
        copy.wait()


def hand_over(*refs):
    given, taken, sems = refs[:7], refs[7:14], refs[14]
    copies = [
        pltpu.make_async_copy(src, dst, sems.at[at])
        for at, (src, dst) in enumerate(zip(given, taken))
    ]
    for copy in copies:
        copy.start()
    for copy in copies:
        copy.wait()


def body(inputs, key_grads, weights, first_moment, second_moment, drift, momentum, global_weights):
    shape = jax.ShapeDtypeStruct
    vmem = pltpu.VMEM
    big = (4 * TOK, COLS)
    piece = (N_ZL, 8, COLS)
    scratch = [
        vmem((TOK, COLS), BF16), vmem((2, TOK, HEAD), F32), vmem((ROWS, COLS), F32),
        vmem((ROWS, COLS), BF16), vmem((ROWS, COLS), BF16), vmem((8, COLS), F32), vmem((8, COLS), F32),
        vmem(big, BF16), vmem(big, BF16), vmem(big, BF16), vmem(big, BF16), vmem(big, BF16),
        vmem(big, BF16), vmem(big, BF16),
        vmem((N_X, TOK, COLS), BF16), vmem((3, TOK, COLS), BF16), vmem((TOK, COLS), F32),
        vmem(big, F32), vmem(big, F32),
        vmem((ROWS, COLS), BF16), vmem((ROWS, COLS), BF16), vmem((ROWS, COLS), BF16),
        vmem((ROWS, COLS), BF16), vmem((ROWS, COLS), BF16), vmem((ROWS, COLS), BF16),
        vmem((N_ZL, N_Y, 8, COLS), F32), vmem((N_Y, N_ZL * 8, COLS), BF16), vmem((N_Y - 1, N_ZL * 8, COLS), BF16),
        vmem(piece, F32), vmem(piece, F32), vmem((N_ZL * 8, COLS), BF16),
        vmem((3, N_ZL * 8, COLS), BF16), vmem((3, N_ZL * 8, COLS), F32), vmem((N_ZL * 8, COLS), BF16),
        vmem((N_Y, N_ZL * 8, COLS), BF16), vmem((8, COLS), F32), vmem((8, COLS), F32), vmem((ROWS, COLS), F32),
        vmem((ROWS, COLS), BF16), vmem((ROWS, COLS), BF16), vmem((TOK, COLS), BF16),
        pltpu.SemaphoreType.DMA((N_REMOTE,)), pltpu.SemaphoreType.DMA((N_REMOTE,)),
        pltpu.SemaphoreType.DMA((len(LOCAL),)), pltpu.SemaphoreType.REGULAR((3,)),
    ]
    outs = (
        shape((1, TOK, COLS), BF16), shape((1, TOK, WIN), BF16), shape((1, ROWS, COLS), F32),
        shape((1, ROWS, COLS), BF16), shape((1, ROWS, COLS), BF16),
        shape((8, COLS), F32), shape((8, COLS), F32),
    )
    anywhere = pl.BlockSpec(memory_space=pl.ANY)
    results = pl.pallas_call(
        kernel,
        out_shape=tuple(vmem(out.shape, out.dtype) for out in outs),
        in_specs=[anywhere] * 9,
        out_specs=[anywhere] * 7,
        scratch_shapes=scratch,
        compiler_params=pltpu.CompilerParams(
            collective_id=0, has_side_effects=True, vmem_limit_bytes=56 * 2**20
        ),
    )(
        inputs, key_grads, weights, first_moment, second_moment,
        drift.reshape(N_ZL, N_Y, 8, COLS), momentum, global_weights, jnp.asarray(rotary_tables()),
    )
    return pl.pallas_call(
        hand_over,
        out_shape=outs,
        in_specs=[anywhere] * 7,
        out_specs=[anywhere] * 7,
        scratch_shapes=[pltpu.SemaphoreType.DMA((7,))],
        compiler_params=pltpu.CompilerParams(vmem_limit_bytes=56 * 2**20),
    )(*[pltpu.with_memory_space_constraint(result, pltpu.VMEM) for result in results])


def solution(mesh):
    split = P("rep", "fsdp", None)
    rows = P(("fsdp", "rep"), None)
    return jax.shard_map(
        body,
        mesh=mesh,
        in_specs=(split,) * 6 + (rows,) * 2,
        out_specs=(split,) * 5 + (rows,) * 2,
        check_vma=False,
    )
```

```python
import functools

import jax
import jax.numpy as jnp
import numpy as np
from jax import lax
from jax.experimental import pallas as pl
from jax.experimental.pallas import tpu as pltpu
from jax.sharding import PartitionSpec as P

HEAD = 128
SEQ = 1024
TOK = 128
ROWS = 256
COLS = 512
WIN = 4096
N_REP = 32
N_X = 4
N_Y = 8
N_ZL = 4

learning_rate = 0.002
beta_one = 0.9
beta_two = 0.95
adam_epsilon = 1e-08
weight_decay = 0.1
outer_rate = 0.7
outer_beta = 0.9
mixing = 0.5
rope_base = 500000.0

F32 = jnp.float32
BF16 = jnp.bfloat16
MESH = pl.DeviceIdType.MESH


def rotary_tables():
    half = HEAD // 2
    freq = rope_base ** (-np.arange(half, dtype=np.float64) * (2.0 / HEAD))
    angles = np.arange(SEQ, dtype=np.float64)[:, None] * freq[None, :]
    cosine, sines = np.cos(angles), np.sin(angles)
    first = np.concatenate([cosine, cosine], axis=1)
    second = np.concatenate([-sines, sines], axis=1)
    both = np.stack([first, second]).astype(np.float32)
    return both.reshape(2, SEQ // TOK, TOK, HEAD).transpose(1, 0, 2, 3).copy()


def rotated_heads(values, tables, sign):
    cosine = tables[0]
    sines = sign * tables[1]
    heads = []
    for head in range(COLS // HEAD):
        part = values[:, head * HEAD : (head + 1) * HEAD]
        heads.append(part * cosine + pltpu.roll(part, HEAD // 2, 1) * sines)
    return jnp.concatenate(heads, axis=1)


SEND = {}
for _at, _names in enumerate((
    ("u",), ("ap",), ("ao",), ("igo",), ("igp",), ("pk",), ("wsib", "wz", "wfwd", "gpsib"),
    ("gosib", "gz"), ("dz",), ("dy",), ("ay",),
)):
    SEND.update({_name: _at for _name in _names})
RECV = {"u": 0, "ap": 1, "ao": 2, "igo": 3, "igp": 4, "pk": 5, "wsib": 6, "wz": 7, "wfwd": 9,
        "gpsib": 10, "gosib": 11, "gz": 12, "dz": 13, "dy": 14, "ay": 15}
N_SEND, N_RECV = 11, 16
LOCAL = {"kg": 0, "tab": 1, "w": 2, "dr": 3, "ap": 4, "ao": 5, "m1": 6, "m2": 6, "mo": 7, "gl": 8,
         "igo": 9, "igp": 9, "mg": 10, "m1o": 10, "m2o": 10, "nm": 11, "ng": 12, "keys": 13}
N_LOCAL = 14
MET_Z, MET_Y, MET_ZL = 0, 1, 2
FAR_FIRST = (4, 3, 5, 2, 6, 1, 7)


def kernel(
    inp, kg, wt, m1, m2, dr, mo, gl, tab,
    keys_out, ig_out, mg_out, m1_out, m2_out, nm_out, ng_out,
    kg_v, tab_v, w_v, m1_v, m2_v, mo_v, gl_v,
    u_all, ap, ao, w_o, w_p, ig_o, ig_p, pk_send, pk_recv, pk_own,
    gp, go, gp_send, gp_recv, go_send, go_recv, gz_send, gz_recv,
    dr_v, dr_low, dr_all, ds, with_base, ds_low, dz, dz_wide, ga_low, gg, nm_v, ng_v, mg_v, m1o_v, m2o_v, keys_v,
    send_sem, recv_sem, local_sem, met,
):
    rep = lax.axis_index("rep")
    fsdp = lax.axis_index("fsdp")
    zl, y = rep // N_Y, rep % N_Y
    zh, x, core = fsdp // 8, (fsdp // 2) % N_X, fsdp % 2

    def chip_x(peer):
        return (rep, zh * 8 + peer * 2 + core)

    def chip_y(peer):
        return (zl * N_Y + peer, fsdp)

    def chip_zl(peer):
        return (peer * N_Y + y, fsdp)

    def at_y(step):
        return chip_y((y + step) % N_Y)

    def at_zl(step):
        return chip_zl((zl + step) % N_ZL)

    sibling = (rep, zh * 8 + x * 2 + (1 - core))
    partner = (rep, (1 - zh) * 8 + x * 2 + core)

    def remote(name, src, dst, device, part=0):
        return pltpu.make_async_remote_copy(
            src_ref=src, dst_ref=dst, send_sem=send_sem.at[SEND[name]],
            recv_sem=recv_sem.at[RECV[name] + part], device_id=device, device_id_type=MESH,
        )

    def local(name, src, dst):
        return pltpu.make_async_copy(src, dst, local_sem.at[LOCAL[name]])

    def arrived(name, size_of):
        remote(name, size_of, size_of, sibling).wait_recv()

    def sent(name, size_of):
        remote(name, size_of, size_of, sibling).wait_send()

    def signal(semaphore, device):
        pl.semaphore_signal(semaphore, inc=1, device_id=device, device_id_type=MESH)

    def wait_for(semaphore, count):
        @pl.when(count > 0)
        def _():
            pl.semaphore_wait(semaphore, count)

    own_rows = pl.ds(pl.multiple_of(core * ROWS, ROWS), ROWS)
    sib_rows = pl.ds(pl.multiple_of((1 - core) * ROWS, ROWS), ROWS)

    def columns(half, chip):
        return pl.ds(pl.multiple_of(half * (WIN // 2) + chip * COLS, COLS), COLS)

    def slot(chip):
        return pl.ds(pl.multiple_of(chip * TOK, TOK), TOK)

    barrier = pltpu.get_barrier_semaphore()
    for step in range(1, N_X):
        signal(barrier, chip_x((x + step) % N_X))
    signal(barrier, sibling)
    for peer in range(1, N_Y):
        @pl.when(peer > y)
        def _():
            signal(barrier, chip_y(peer))
    for peer in range(1, N_ZL):
        @pl.when(peer > zl)
        def _():
            signal(barrier, chip_zl(peer))

    @pl.when(zh == 0)
    def _():
        signal(barrier, partner)

    loads = {
        "kg": local("kg", kg.at[0], kg_v),
        "tab": local("tab", tab.at[fsdp % 8], tab_v),
        "w": local("w", wt.at[0], w_v),
        "ap": local("ap", inp.at[0, :, columns(1 - zh, x)], ap.at[slot(x)]),
        "ao": local("ao", inp.at[0, :, columns(zh, x)], ao.at[slot(x)]),
        "dr": local("dr", dr, dr_v),
        "m1": local("m1", m1.at[0], m1_v),
        "m2": local("m2", m2.at[0], m2_v),
        "mo": local("mo", mo, mo_v),
        "gl": local("gl", gl, gl_v),
    }
    for name in ("kg", "tab", "w", "dr"):
        loads[name].start()

    pl.semaphore_wait(barrier, N_X + y + zl + zh)

    @pl.when(zh == 1)
    def _():
        signal(met.at[MET_Z], partner)

    for peer in range(N_Y - 1):
        @pl.when(peer < y)
        def _():
            signal(met.at[MET_Y], chip_y(peer))
    for peer in range(N_ZL - 1):
        @pl.when(peer < zl)
        def _():
            signal(met.at[MET_ZL], chip_zl(peer))

    for name in ("ap", "ao", "m1", "m2", "mo", "gl"):
        loads[name].start()

    loads["kg"].wait()
    loads["tab"].wait()
    tables = (tab_v[0], tab_v[1])
    u_all[slot(x), :] = rotated_heads(kg_v[...].astype(F32), tables, -1.0).astype(BF16)
    loads["w"].wait()
    w_o[own_rows, :] = w_v[...].astype(BF16)

    loads["dr"].wait()
    for peer in range(N_Y):
        dr_low[peer] = dr_v[:, peer].reshape(N_ZL * 8, COLS).astype(BF16)

    ahead = zl < N_ZL // 2
    behind = jnp.logical_not(ahead)

    def half_rows(half):
        return pl.ds(pl.multiple_of(core * ROWS + half * (ROWS // 2), ROWS // 2), ROWS // 2)

    wz = [
        remote("wz", w_o.at[half_rows(half)], w_p.at[half_rows(half)], partner, half)
        for half in range(2)
    ]
    wsib = remote("wsib", w_o.at[own_rows], w_o.at[own_rows], sibling)

    @pl.when(zh == 1)
    def _():
        wz[0].start()
        wz[1].start()

    wsib.start()

    def to_x(name, src, dst):
        return [remote(name, src(peer), dst(peer), chip_x(peer)) for peer in range(N_X)]

    def each_peer(act):
        for peer in range(N_X):
            pl.when(peer != x)(functools.partial(act, peer))

    u_copy = to_x("u", lambda peer: u_all.at[slot(x)], lambda peer: u_all.at[slot(x)])
    ap_copy = to_x(
        "ap", lambda peer: inp.at[0, :, columns(1 - zh, peer)], lambda peer: ap.at[slot(x)]
    )
    ao_copy = to_x(
        "ao", lambda peer: inp.at[0, :, columns(zh, peer)], lambda peer: ao.at[slot(x)]
    )

    each_peer(lambda peer: u_copy[peer].start())
    each_peer(lambda peer: ap_copy[peer].start())

    dy_copy = [
        remote("dy", dr_low.at[(y + e) % N_Y], dr_all.at[e - 1], at_y(e))
        for e in range(1, N_Y)
    ]
    wait_for(met.at[MET_Y], N_Y - 1 - y)
    for e in FAR_FIRST:
        dy_copy[e - 1].start()

    each_peer(lambda peer: ao_copy[peer].start())

    @pl.when(zh == 0)
    def _():
        pl.semaphore_wait(met.at[MET_Z], 1)
        wz[0].start()
        wz[1].start()

    wsib.wait_recv()
    arrived("u", pk_recv)
    ig_o[...] = lax.dot_general(
        u_all[...], w_o[...], (((1,), (1,)), ((), ())), preferred_element_type=F32
    ).astype(BF16)
    igo_copy = to_x(
        "igo", lambda peer: ig_o.at[slot(peer)], lambda peer: ig_out.at[0, :, columns(zh, x)]
    )
    each_peer(lambda peer: igo_copy[peer].start())
    local("igo", ig_o.at[slot(x)], ig_out.at[0, :, columns(zh, x)]).start()

    arrived("dy", dr_all)
    total = dr_v[:, y].reshape(N_ZL * 8, COLS)
    for e in range(N_Y - 1):
        total = total + dr_all[e].astype(F32)
    ds[...] = total.reshape(N_ZL, 8, COLS)
    loads["mo"].wait()
    loads["gl"].wait()
    with_base[...] = ds[...]
    base = gl_v[...] - (outer_rate * outer_beta * outer_beta) * mo_v[...]
    with_base[zl] = ds[zl] - (N_REP / (outer_rate * (1.0 + outer_beta))) * base
    ds_low[...] = with_base[...].reshape(N_ZL * 8, COLS).astype(BF16)
    dz_copy = [
        remote("dz", ds_low, dz.at[f - 1], at_zl(f)) for f in range(1, N_ZL)
    ]
    wait_for(met.at[MET_ZL], N_ZL - 1 - zl)
    for copy in dz_copy:
        copy.start()

    loads["ap"].wait()
    arrived("ap", pk_recv)
    gp[...] = lax.dot_general(
        ap[...], u_all[...], (((0,), (0,)), ((), ())), preferred_element_type=F32
    )
    gp_send[...] = gp[sib_rows, :].astype(BF16)
    gpsib = remote("gpsib", gp_send, gp_recv, sibling)
    gpsib.start()

    gpsib.wait_recv()
    gz_send[...] = (gp[own_rows, :] + gp_recv[...].astype(F32)).astype(BF16)
    gz = remote("gz", gz_send, gz_recv, partner)

    @pl.when(zh == 1)
    def _():
        gz.start()

    wfwd = [
        remote("wfwd", w_p.at[half_rows(half)], w_p.at[half_rows(half)], sibling)
        for half in range(2)
    ]
    for half in range(2):
        wz[half].wait_recv()
        wfwd[half].start()
    arrived("wfwd", gz_send)

    ig_p[...] = lax.dot_general(
        u_all[...], w_p[...], (((1,), (1,)), ((), ())), preferred_element_type=F32
    ).astype(BF16)
    igp_copy = to_x(
        "igp", lambda peer: ig_p.at[slot(peer)], lambda peer: ig_out.at[0, :, columns(1 - zh, x)]
    )
    each_peer(lambda peer: igp_copy[peer].start())
    local("igp", ig_p.at[slot(x)], ig_out.at[0, :, columns(1 - zh, x)]).start()

    loads["ao"].wait()
    arrived("ao", pk_recv)
    go[...] = lax.dot_general(
        ao[...], u_all[...], (((0,), (0,)), ((), ())), preferred_element_type=F32
    )
    go_send[...] = go[sib_rows, :].astype(BF16)
    gosib = remote("gosib", go_send, go_recv, sibling)
    gosib.start()

    pk_copy = to_x("pk", lambda peer: pk_send.at[peer], lambda peer: pk_recv.at[(peer - x + 3) % 4])
    for peer in range(N_X):
        part = jnp.dot(ao[slot(peer), :], w_o[...], preferred_element_type=F32)
        part += jnp.dot(ap[slot(peer), :], w_p[...], preferred_element_type=F32)

        @pl.when(peer == x)
        def _():
            pk_own[...] = part

        @pl.when(peer != x)
        def _():
            pk_send[peer] = part.astype(BF16)
            pk_copy[peer].start()

    @pl.when(zh == 0)
    def _():
        gz.start()

    arrived("dz", dz)
    total = with_base[...].reshape(N_ZL * 8, COLS)
    for step in range(N_ZL - 1):
        total = total + dz[step].astype(F32)
    ga_low[...] = ((-outer_rate * (1.0 + outer_beta) / N_REP) * total).astype(BF16)
    ay_copy = [remote("ay", ga_low, gg.at[y], at_y(e)) for e in range(1, N_Y)]
    for e in FAR_FIRST:
        ay_copy[e - 1].start()
    gg[y] = ga_low[...]
    own_piece = pl.ds(pl.multiple_of(zl * 8, 8), 8)
    own_total = ds[zl]
    for step in range(N_ZL - 1):
        dz_wide[step] = dz[step].astype(F32)
        own_total = own_total + dz_wide[step, own_piece, :]
    mean_drift = own_total / N_REP
    moment = outer_beta * mo_v[...] + mean_drift
    nm_v[...] = moment
    ng_v[...] = gl_v[...] - outer_rate * (mean_drift + outer_beta * moment)
    outs = [local("nm", nm_v, nm_out)]
    outs[-1].start()
    outs.append(local("ng", ng_v, ng_out))
    outs[-1].start()

    local("m1", u_all, u_all).wait()
    gosib.wait_recv()
    arrived("ay", dr_all)
    gz.wait_recv()

    for zone in range(N_ZL):
        rows = pl.ds(zone * 64, 64)
        gradient = (
            go[pl.ds(pl.multiple_of(core * ROWS + zone * 64, 64), 64), :]
            + go_recv[rows, :].astype(F32)
            + gz_recv[rows, :].astype(F32)
        )
        master = w_v[rows, :]
        spread = gg[:, pl.ds(zone * 8, 8), :].astype(F32).reshape(64, COLS)
        moment_one = beta_one * m1_v[rows, :].astype(F32) + (1.0 - beta_one) * gradient
        moment_two = (
            beta_two * m2_v[rows, :].astype(F32) + (1.0 - beta_two) * gradient * gradient
        )
        stepped = master - learning_rate * (
            moment_one / (jnp.sqrt(moment_two) + adam_epsilon) + weight_decay * master
        )
        mg_v[rows, :] = mixing * stepped + (1.0 - mixing) * spread
        m1o_v[rows, :] = moment_one.astype(BF16)
        m2o_v[rows, :] = moment_two.astype(BF16)
    for name, src, dst in (("mg", mg_v, mg_out), ("m1o", m1o_v, m1_out), ("m2o", m2o_v, m2_out)):
        local(name, src, dst.at[0]).start()

    arrived("pk", pk_recv)
    projected = pk_own[...]
    for step in range(3):
        projected = projected + pk_recv[step].astype(F32)
    keys_v[...] = rotated_heads(projected, tables, 1.0).astype(BF16)
    outs.append(local("keys", keys_v, keys_out.at[0]))
    outs[-1].start()

    arrived("igo", pk_recv)
    arrived("igp", pk_recv)
    for name in ("u", "ap", "ao", "igo", "igp", "pk"):
        sent(name, pk_recv)
    sent("wsib", gp)
    sent("gosib", u_all)
    sent("dz", dz)
    sent("dy", dr_all)
    sent("ay", dr_all)
    local("igo", gz_send, gz_send).wait()
    local("mg", gp, gp).wait()
    for copy in outs:
        copy.wait()


def hand_over(*refs):
    given, taken, sems = refs[:7], refs[7:14], refs[14]
    copies = [
        pltpu.make_async_copy(src, dst, sems.at[at])
        for at, (src, dst) in enumerate(zip(given, taken))
    ]
    for copy in copies:
        copy.start()
    for copy in copies:
        copy.wait()


def body(inputs, key_grads, weights, first_moment, second_moment, drift, momentum, global_weights):
    shape = jax.ShapeDtypeStruct
    vmem = pltpu.VMEM
    big = (4 * TOK, COLS)
    piece = (N_ZL, 8, COLS)
    scratch = [
        vmem((TOK, COLS), BF16), vmem((2, TOK, HEAD), F32), vmem((ROWS, COLS), F32),
        vmem((ROWS, COLS), BF16), vmem((ROWS, COLS), BF16), vmem((8, COLS), F32), vmem((8, COLS), F32),
        vmem(big, BF16), vmem(big, BF16), vmem(big, BF16), vmem(big, BF16), vmem(big, BF16),
        vmem(big, BF16), vmem(big, BF16),
        vmem((N_X, TOK, COLS), BF16), vmem((3, TOK, COLS), BF16), vmem((TOK, COLS), F32),
        vmem(big, F32), vmem(big, F32),
        vmem((ROWS, COLS), BF16), vmem((ROWS, COLS), BF16), vmem((ROWS, COLS), BF16),
        vmem((ROWS, COLS), BF16), vmem((ROWS, COLS), BF16), vmem((ROWS, COLS), BF16),
        vmem((N_ZL, N_Y, 8, COLS), F32), vmem((N_Y, N_ZL * 8, COLS), BF16), vmem((N_Y - 1, N_ZL * 8, COLS), BF16),
        vmem(piece, F32), vmem(piece, F32), vmem((N_ZL * 8, COLS), BF16),
        vmem((3, N_ZL * 8, COLS), BF16), vmem((3, N_ZL * 8, COLS), F32), vmem((N_ZL * 8, COLS), BF16),
        vmem((N_Y, N_ZL * 8, COLS), BF16), vmem((8, COLS), F32), vmem((8, COLS), F32), vmem((ROWS, COLS), F32),
        vmem((ROWS, COLS), BF16), vmem((ROWS, COLS), BF16), vmem((TOK, COLS), BF16),
        pltpu.SemaphoreType.DMA((N_SEND,)), pltpu.SemaphoreType.DMA((N_RECV,)),
        pltpu.SemaphoreType.DMA((N_LOCAL,)), pltpu.SemaphoreType.REGULAR((3,)),
    ]
    outs = (
        shape((1, TOK, COLS), BF16), shape((1, TOK, WIN), BF16), shape((1, ROWS, COLS), F32),
        shape((1, ROWS, COLS), BF16), shape((1, ROWS, COLS), BF16),
        shape((8, COLS), F32), shape((8, COLS), F32),
    )
    anywhere = pl.BlockSpec(memory_space=pl.ANY)
    results = pl.pallas_call(
        kernel,
        out_shape=tuple(vmem(out.shape, out.dtype) for out in outs),
        in_specs=[anywhere] * 9,
        out_specs=[anywhere] * 7,
        scratch_shapes=scratch,
        compiler_params=pltpu.CompilerParams(
            collective_id=0, has_side_effects=True, vmem_limit_bytes=56 * 2**20
        ),
    )(
        inputs, key_grads, weights, first_moment, second_moment,
        drift.reshape(N_ZL, N_Y, 8, COLS), momentum, global_weights, jnp.asarray(rotary_tables()),
    )
    return pl.pallas_call(
        hand_over,
        out_shape=outs,
        in_specs=[anywhere] * 7,
        out_specs=[anywhere] * 7,
        scratch_shapes=[pltpu.SemaphoreType.DMA((7,))],
        compiler_params=pltpu.CompilerParams(vmem_limit_bytes=56 * 2**20),
    )(*[pltpu.with_memory_space_constraint(result, pltpu.VMEM) for result in results])


def solution(mesh):
    split = P("rep", "fsdp", None)
    rows = P(("fsdp", "rep"), None)
    return jax.shard_map(
        body,
        mesh=mesh,
        in_specs=(split,) * 6 + (rows,) * 2,
        out_specs=(split,) * 5 + (rows,) * 2,
        check_vma=False,
    )
```

```python
import functools

import jax
import jax.numpy as jnp
import numpy as np
from jax import lax
from jax.experimental import pallas as pl
from jax.experimental.pallas import tpu as pltpu
from jax.sharding import PartitionSpec as P

HEAD = 128
SEQ = 1024
TOK = 128
ROWS = 256
COLS = 512
WIN = 4096
N_REP = 32
N_X = 4
N_Y = 8
N_ZL = 4

learning_rate = 0.002
beta_one = 0.9
beta_two = 0.95
adam_epsilon = 1e-08
weight_decay = 0.1
outer_rate = 0.7
outer_beta = 0.9
mixing = 0.5
rope_base = 500000.0

F32 = jnp.float32
BF16 = jnp.bfloat16
MESH = pl.DeviceIdType.MESH


def rotary_tables():
    half = HEAD // 2
    freq = rope_base ** (-np.arange(half, dtype=np.float64) * (2.0 / HEAD))
    angles = np.arange(SEQ, dtype=np.float64)[:, None] * freq[None, :]
    cosine, sines = np.cos(angles), np.sin(angles)
    first = np.concatenate([cosine, cosine], axis=1)
    second = np.concatenate([-sines, sines], axis=1)
    both = np.stack([first, second]).astype(np.float32)
    return both.reshape(2, SEQ // TOK, TOK, HEAD).transpose(1, 0, 2, 3).copy()


def rotated_heads(values, tables, sign):
    cosine = tables[0]
    sines = sign * tables[1]
    heads = []
    for head in range(COLS // HEAD):
        part = values[:, head * HEAD : (head + 1) * HEAD]
        heads.append(part * cosine + pltpu.roll(part, HEAD // 2, 1) * sines)
    return jnp.concatenate(heads, axis=1)


SEND = {}
for _at, _names in enumerate((
    ("u",), ("ap",), ("ao",), ("igo",), ("igp",), ("pk",), ("wsib", "wz", "wfwd", "gpsib"),
    ("gosib", "gz"), ("dz",), ("dy",), ("ay",),
)):
    SEND.update({_name: _at for _name in _names})
RECV = {"u": 0, "ap": 1, "ao": 2, "igo": 3, "igp": 4, "pk": 5, "wsib": 6, "wz": 7, "wfwd": 9,
        "gpsib": 10, "gosib": 11, "gz": 12, "dz": 13, "dy": 14, "ay": 15}
N_SEND, N_RECV = 11, 16
LOCAL = {"kg": 0, "tab": 1, "w": 2, "dr": 3, "ap": 4, "ao": 5, "m1": 6, "m2": 6, "mo": 7, "gl": 8,
         "igo": 9, "igp": 9}
N_LOCAL = 10
MET_Z, MET_Y, MET_ZL = 0, 1, 2
FAR_FIRST = (4, 3, 5, 2, 6, 1, 7)


def kernel(
    inp, kg, wt, m1, m2, dr, mo, gl, tab,
    keys_out, ig_out, mg_out, m1_out, m2_out, nm_out, ng_out,
    kg_v, tab_v, w_v, m1_v, m2_v, mo_v, gl_v,
    u_all, ap, ao, w_o, w_p, ig_o, ig_p, pk_send, pk_recv, pk_own,
    gp, go, gp_send, gp_recv, go_send, go_recv, gz_send, gz_recv,
    dr_v, dr_low, dr_all, ds, with_base, ds_low, dz, dz_wide, ga_low, gg,
    send_sem, recv_sem, local_sem, met,
):
    rep = lax.axis_index("rep")
    fsdp = lax.axis_index("fsdp")
    zl, y = rep // N_Y, rep % N_Y
    zh, x, core = fsdp // 8, (fsdp // 2) % N_X, fsdp % 2

    def chip_x(peer):
        return (rep, zh * 8 + peer * 2 + core)

    def chip_y(peer):
        return (zl * N_Y + peer, fsdp)

    def chip_zl(peer):
        return (peer * N_Y + y, fsdp)

    def at_y(step):
        return chip_y((y + step) % N_Y)

    def at_zl(step):
        return chip_zl((zl + step) % N_ZL)

    sibling = (rep, zh * 8 + x * 2 + (1 - core))
    partner = (rep, (1 - zh) * 8 + x * 2 + core)

    def remote(name, src, dst, device, part=0):
        return pltpu.make_async_remote_copy(
            src_ref=src, dst_ref=dst, send_sem=send_sem.at[SEND[name]],
            recv_sem=recv_sem.at[RECV[name] + part], device_id=device, device_id_type=MESH,
        )

    def local(name, src, dst):
        return pltpu.make_async_copy(src, dst, local_sem.at[LOCAL[name]])

    def arrived(name, size_of):
        remote(name, size_of, size_of, sibling).wait_recv()

    def sent(name, size_of):
        remote(name, size_of, size_of, sibling).wait_send()

    def signal(semaphore, device):
        pl.semaphore_signal(semaphore, inc=1, device_id=device, device_id_type=MESH)

    def wait_for(semaphore, count):
        @pl.when(count > 0)
        def _():
            pl.semaphore_wait(semaphore, count)

    own_rows = pl.ds(pl.multiple_of(core * ROWS, ROWS), ROWS)
    sib_rows = pl.ds(pl.multiple_of((1 - core) * ROWS, ROWS), ROWS)

    def columns(half, chip):
        return pl.ds(pl.multiple_of(half * (WIN // 2) + chip * COLS, COLS), COLS)

    def slot(chip):
        return pl.ds(pl.multiple_of(chip * TOK, TOK), TOK)

    barrier = pltpu.get_barrier_semaphore()
    for step in range(1, N_X):
        signal(barrier, chip_x((x + step) % N_X))
    signal(barrier, sibling)
    for peer in range(1, N_Y):
        @pl.when(peer > y)
        def _():
            signal(barrier, chip_y(peer))
    for peer in range(1, N_ZL):
        @pl.when(peer > zl)
        def _():
            signal(barrier, chip_zl(peer))

    @pl.when(zh == 0)
    def _():
        signal(barrier, partner)

    loads = {
        "kg": local("kg", kg.at[0], kg_v),
        "tab": local("tab", tab.at[fsdp % 8], tab_v),
        "w": local("w", wt.at[0], w_v),
        "ap": local("ap", inp.at[0, :, columns(1 - zh, x)], ap.at[slot(x)]),
        "ao": local("ao", inp.at[0, :, columns(zh, x)], ao.at[slot(x)]),
        "dr": local("dr", dr, dr_v),
        "m1": local("m1", m1.at[0], m1_v),
        "m2": local("m2", m2.at[0], m2_v),
        "mo": local("mo", mo, mo_v),
        "gl": local("gl", gl, gl_v),
    }
    for name in ("kg", "tab", "w", "dr"):
        loads[name].start()

    pl.semaphore_wait(barrier, N_X + y + zl + zh)

    @pl.when(zh == 1)
    def _():
        signal(met.at[MET_Z], partner)

    for peer in range(N_Y - 1):
        @pl.when(peer < y)
        def _():
            signal(met.at[MET_Y], chip_y(peer))
    for peer in range(N_ZL - 1):
        @pl.when(peer < zl)
        def _():
            signal(met.at[MET_ZL], chip_zl(peer))

    for name in ("ap", "ao", "m1", "m2", "mo", "gl"):
        loads[name].start()

    loads["kg"].wait()
    loads["tab"].wait()
    tables = (tab_v[0], tab_v[1])
    u_all[slot(x), :] = rotated_heads(kg_v[...].astype(F32), tables, -1.0).astype(BF16)
    loads["w"].wait()
    w_o[own_rows, :] = w_v[...].astype(BF16)

    loads["dr"].wait()
    for peer in range(N_Y):
        dr_low[peer] = dr_v[:, peer].reshape(N_ZL * 8, COLS).astype(BF16)

    ahead = zl < N_ZL // 2
    behind = jnp.logical_not(ahead)

    def half_rows(half):
        return pl.ds(pl.multiple_of(core * ROWS + half * (ROWS // 2), ROWS // 2), ROWS // 2)

    wz = [
        remote("wz", w_o.at[half_rows(half)], w_p.at[half_rows(half)], partner, half)
        for half in range(2)
    ]
    wsib = remote("wsib", w_o.at[own_rows], w_o.at[own_rows], sibling)

    @pl.when(zh == 1)
    def _():
        wz[0].start()
        wz[1].start()

    wsib.start()

    def to_x(name, src, dst):
        return [remote(name, src(peer), dst(peer), chip_x(peer)) for peer in range(N_X)]

    def each_peer(act):
        for peer in range(N_X):
            pl.when(peer != x)(functools.partial(act, peer))

    u_copy = to_x("u", lambda peer: u_all.at[slot(x)], lambda peer: u_all.at[slot(x)])
    ap_copy = to_x(
        "ap", lambda peer: inp.at[0, :, columns(1 - zh, peer)], lambda peer: ap.at[slot(x)]
    )
    ao_copy = to_x(
        "ao", lambda peer: inp.at[0, :, columns(zh, peer)], lambda peer: ao.at[slot(x)]
    )

    each_peer(lambda peer: u_copy[peer].start())
    each_peer(lambda peer: ap_copy[peer].start())

    dy_copy = [
        remote("dy", dr_low.at[(y + e) % N_Y], dr_all.at[e - 1], at_y(e))
        for e in range(1, N_Y)
    ]
    wait_for(met.at[MET_Y], N_Y - 1 - y)
    for e in FAR_FIRST:
        dy_copy[e - 1].start()

    each_peer(lambda peer: ao_copy[peer].start())

    @pl.when(zh == 0)
    def _():
        pl.semaphore_wait(met.at[MET_Z], 1)
        wz[0].start()
        wz[1].start()

    wsib.wait_recv()
    arrived("u", pk_recv)
    ig_o[...] = lax.dot_general(
        u_all[...], w_o[...], (((1,), (1,)), ((), ())), preferred_element_type=F32
    ).astype(BF16)
    igo_copy = to_x(
        "igo", lambda peer: ig_o.at[slot(peer)], lambda peer: ig_out.at[0, :, columns(zh, x)]
    )
    each_peer(lambda peer: igo_copy[peer].start())
    local("igo", ig_o.at[slot(x)], ig_out.at[0, :, columns(zh, x)]).start()

    arrived("dy", dr_all)
    total = dr_v[:, y].reshape(N_ZL * 8, COLS)
    for e in range(N_Y - 1):
        total = total + dr_all[e].astype(F32)
    ds[...] = total.reshape(N_ZL, 8, COLS)
    loads["mo"].wait()
    loads["gl"].wait()
    with_base[...] = ds[...]
    base = gl_v[...] - (outer_rate * outer_beta * outer_beta) * mo_v[...]
    with_base[zl] = ds[zl] - (N_REP / (outer_rate * (1.0 + outer_beta))) * base
    ds_low[...] = with_base[...].reshape(N_ZL * 8, COLS).astype(BF16)
    dz_copy = [
        remote("dz", ds_low, dz.at[f - 1], at_zl(f)) for f in range(1, N_ZL)
    ]
    wait_for(met.at[MET_ZL], N_ZL - 1 - zl)
    for copy in dz_copy:
        copy.start()

    loads["ap"].wait()
    arrived("ap", pk_recv)
    gp[...] = lax.dot_general(
        ap[...], u_all[...], (((0,), (0,)), ((), ())), preferred_element_type=F32
    )
    gp_send[...] = gp[sib_rows, :].astype(BF16)
    gpsib = remote("gpsib", gp_send, gp_recv, sibling)
    gpsib.start()

    gpsib.wait_recv()
    gz_send[...] = (gp[own_rows, :] + gp_recv[...].astype(F32)).astype(BF16)
    gz = remote("gz", gz_send, gz_recv, partner)

    @pl.when(zh == 1)
    def _():
        gz.start()

    wfwd = [
        remote("wfwd", w_p.at[half_rows(half)], w_p.at[half_rows(half)], sibling)
        for half in range(2)
    ]
    for half in range(2):
        wz[half].wait_recv()
        wfwd[half].start()
    arrived("wfwd", gz_send)

    ig_p[...] = lax.dot_general(
        u_all[...], w_p[...], (((1,), (1,)), ((), ())), preferred_element_type=F32
    ).astype(BF16)
    igp_copy = to_x(
        "igp", lambda peer: ig_p.at[slot(peer)], lambda peer: ig_out.at[0, :, columns(1 - zh, x)]
    )
    each_peer(lambda peer: igp_copy[peer].start())
    local("igp", ig_p.at[slot(x)], ig_out.at[0, :, columns(1 - zh, x)]).start()

    loads["ao"].wait()
    arrived("ao", pk_recv)
    go[...] = lax.dot_general(
        ao[...], u_all[...], (((0,), (0,)), ((), ())), preferred_element_type=F32
    )
    go_send[...] = go[sib_rows, :].astype(BF16)
    gosib = remote("gosib", go_send, go_recv, sibling)
    gosib.start()

    pk_copy = to_x("pk", lambda peer: pk_send.at[peer], lambda peer: pk_recv.at[(peer - x + 3) % 4])
    for peer in range(N_X):
        part = jnp.dot(ao[slot(peer), :], w_o[...], preferred_element_type=F32)
        part += jnp.dot(ap[slot(peer), :], w_p[...], preferred_element_type=F32)

        @pl.when(peer == x)
        def _():
            pk_own[...] = part

        @pl.when(peer != x)
        def _():
            pk_send[peer] = part.astype(BF16)
            pk_copy[peer].start()

    @pl.when(zh == 0)
    def _():
        gz.start()

    arrived("dz", dz)
    total = with_base[...].reshape(N_ZL * 8, COLS)
    for step in range(N_ZL - 1):
        total = total + dz[step].astype(F32)
    ga_low[...] = ((-outer_rate * (1.0 + outer_beta) / N_REP) * total).astype(BF16)
    ay_copy = [remote("ay", ga_low, gg.at[y], at_y(e)) for e in range(1, N_Y)]
    for e in FAR_FIRST:
        ay_copy[e - 1].start()
    gg[y] = ga_low[...]
    own_piece = pl.ds(pl.multiple_of(zl * 8, 8), 8)
    own_total = ds[zl]
    for step in range(N_ZL - 1):
        dz_wide[step] = dz[step].astype(F32)
        own_total = own_total + dz_wide[step, own_piece, :]
    mean_drift = own_total / N_REP
    moment = outer_beta * mo_v[...] + mean_drift
    nm_out[...] = moment
    ng_out[...] = gl_v[...] - outer_rate * (mean_drift + outer_beta * moment)

    local("m1", u_all, u_all).wait()
    gosib.wait_recv()
    def finish_keys():
        arrived("pk", pk_recv)
        projected = pk_own[...]
        for step in range(3):
            projected = projected + pk_recv[step].astype(F32)
        keys_out[0] = rotated_heads(projected, tables, 1.0).astype(BF16)

    arrived("ay", dr_all)
    gz.wait_recv()

    for zone in range(N_ZL):
        rows = pl.ds(zone * 64, 64)
        gradient = (
            go[pl.ds(pl.multiple_of(core * ROWS + zone * 64, 64), 64), :]
            + go_recv[rows, :].astype(F32)
            + gz_recv[rows, :].astype(F32)
        )
        master = w_v[rows, :]
        spread = gg[:, pl.ds(zone * 8, 8), :].astype(F32).reshape(64, COLS)
        moment_one = beta_one * m1_v[rows, :].astype(F32) + (1.0 - beta_one) * gradient
        moment_two = (
            beta_two * m2_v[rows, :].astype(F32) + (1.0 - beta_two) * gradient * gradient
        )
        stepped = master - learning_rate * (
            moment_one / (jnp.sqrt(moment_two) + adam_epsilon) + weight_decay * master
        )
        mg_out[0, rows, :] = mixing * stepped + (1.0 - mixing) * spread
        m1_out[0, rows, :] = moment_one.astype(BF16)
        m2_out[0, rows, :] = moment_two.astype(BF16)

    finish_keys()

    arrived("igo", pk_recv)
    arrived("igp", pk_recv)
    for name in ("u", "ap", "ao", "igo", "igp", "pk"):
        sent(name, pk_recv)
    sent("wsib", gp)
    sent("gosib", u_all)
    sent("dz", dz)
    sent("dy", dr_all)
    sent("ay", dr_all)
    local("igo", gz_send, gz_send).wait()


def hand_over(*refs):
    given, taken, sems = refs[:7], refs[7:14], refs[14]
    copies = [
        pltpu.make_async_copy(src, dst, sems.at[at])
        for at, (src, dst) in enumerate(zip(given, taken))
    ]
    for copy in copies:
        copy.start()
    for copy in copies:
        copy.wait()


def body(inputs, key_grads, weights, first_moment, second_moment, drift, momentum, global_weights):
    shape = jax.ShapeDtypeStruct
    vmem = pltpu.VMEM
    big = (4 * TOK, COLS)
    piece = (N_ZL, 8, COLS)
    scratch = [
        vmem((TOK, COLS), BF16), vmem((2, TOK, HEAD), F32), vmem((ROWS, COLS), F32),
        vmem((ROWS, COLS), BF16), vmem((ROWS, COLS), BF16), vmem((8, COLS), F32), vmem((8, COLS), F32),
        vmem(big, BF16), vmem(big, BF16), vmem(big, BF16), vmem(big, BF16), vmem(big, BF16),
        vmem(big, BF16), vmem(big, BF16),
        vmem((N_X, TOK, COLS), BF16), vmem((3, TOK, COLS), BF16), vmem((TOK, COLS), F32),
        vmem(big, F32), vmem(big, F32),
        vmem((ROWS, COLS), BF16), vmem((ROWS, COLS), BF16), vmem((ROWS, COLS), BF16),
        vmem((ROWS, COLS), BF16), vmem((ROWS, COLS), BF16), vmem((ROWS, COLS), BF16),
        vmem((N_ZL, N_Y, 8, COLS), F32), vmem((N_Y, N_ZL * 8, COLS), BF16), vmem((N_Y - 1, N_ZL * 8, COLS), BF16),
        vmem(piece, F32), vmem(piece, F32), vmem((N_ZL * 8, COLS), BF16),
        vmem((3, N_ZL * 8, COLS), BF16), vmem((3, N_ZL * 8, COLS), F32), vmem((N_ZL * 8, COLS), BF16),
        vmem((N_Y, N_ZL * 8, COLS), BF16),
        pltpu.SemaphoreType.DMA((N_SEND,)), pltpu.SemaphoreType.DMA((N_RECV,)),
        pltpu.SemaphoreType.DMA((N_LOCAL,)), pltpu.SemaphoreType.REGULAR((3,)),
    ]
    outs = (
        shape((1, TOK, COLS), BF16), shape((1, TOK, WIN), BF16), shape((1, ROWS, COLS), F32),
        shape((1, ROWS, COLS), BF16), shape((1, ROWS, COLS), BF16),
        shape((8, COLS), F32), shape((8, COLS), F32),
    )
    anywhere = pl.BlockSpec(memory_space=pl.ANY)
    results = pl.pallas_call(
        kernel,
        out_shape=tuple(vmem(out.shape, out.dtype) for out in outs),
        in_specs=[anywhere] * 9,
        out_specs=[pl.BlockSpec(memory_space=pltpu.VMEM)] * 7,
        scratch_shapes=scratch,
        compiler_params=pltpu.CompilerParams(
            collective_id=0, has_side_effects=True, vmem_limit_bytes=56 * 2**20
        ),
    )(
        inputs, key_grads, weights, first_moment, second_moment,
        drift.reshape(N_ZL, N_Y, 8, COLS), momentum, global_weights, jnp.asarray(rotary_tables()),
    )
    return pl.pallas_call(
        hand_over,
        out_shape=outs,
        in_specs=[anywhere] * 7,
        out_specs=[anywhere] * 7,
        scratch_shapes=[pltpu.SemaphoreType.DMA((7,))],
        compiler_params=pltpu.CompilerParams(vmem_limit_bytes=56 * 2**20),
    )(*[pltpu.with_memory_space_constraint(result, pltpu.VMEM) for result in results])


def solution(mesh):
    split = P("rep", "fsdp", None)
    rows = P(("fsdp", "rep"), None)
    return jax.shard_map(
        body,
        mesh=mesh,
        in_specs=(split,) * 6 + (rows,) * 2,
        out_specs=(split,) * 5 + (rows,) * 2,
        check_vma=False,
    )
```
